32 devices in a mesh: group: 2 (over x), row: 8 (over z, y), expert: 2 (over core).
Axes of the slice: x: 2, y: 2, z: 4, core: 2. Of those that a mesh axis runs over, the one named last changes fastest.
Arguments:
- tokens: bfloat16 [2, 128, 128, 1024], P('group', ('row', 'expert')), parts along dimension 0, may hold values from -30 to 30
- ln_first: float32 [1024], replicated, may hold values from 0.5 to 1.5
- spec_first: bfloat16 [2, 8, 128, 128], replicated, may hold values from -0.375 to 0.375
- spec_second: bfloat16 [2, 8, 128, 128], replicated, may hold values from -0.375 to 0.375
- spec_bias: float32 [2, 1024], replicated, may hold values from -3 to 3
- ln_second: float32 [1024], replicated, may hold values from 0.5 to 1.5
- routing: int32 [2, 128, 128, 4], P('group', ('row', 'expert')), parts along dimension 0, may hold values from 0 to 3, as said below
- combine: float32 [2, 128, 128, 4], P('group', ('row', 'expert')), parts along dimension 0, may hold values from 0.1 to 0.6
- up_weight: bfloat16 [8, 1024, 1536], P('row'), may hold values from -0.1875 to 0.1875
- down_weight: bfloat16 [8, 1536, 1024], P('row'), may hold values from -0.109375 to 0.109375
Outputs:
- block_out: bfloat16 [2, 128, 128, 1024], P('group', ('row', 'expert')), parts along dimension 0
The draws below stay inside these ranges and needn't reach their ends.
There are 2 independent parts, one for each index of `group`. The reference program is written for one: setup_inputs(seed, part) draws one part's arguments, and reference() takes and returns one part's arrays. A program takes and returns all parts, laid end to end along the dimension named above; an argument that names none is the same for every part. Nothing has to cross between parts.
Inputs may be any that keep to these rules, and one draw needn't show every extreme that they name: `routing`: each token names 4 different experts, and the 1024 tokens held by each index of row+expert name every expert exactly 1024 times.
All inputs are finite; a program needn't handle non-finite values.
Results may differ from the reference program's by a relative error of at most 0.006.
Values may be sent and summed in bfloat16 or wider, within the bound.
No kernel may reach another device: no remote copies, remote signals or barrier semaphores. Data moves between devices by JAX's collectives and lax.ppermute only.
A program may use at most 128 MiB of HBM per device.

```python
import math
import jax
import jax.numpy as jnp
from jax import lax

GRID = 128
D = 1024
FF = 3072
NB = 8
TOPK = 4
GRIDS = 1
TOK_DEV = 1024
EXPERTS = 4


def draw_tokens(key, part):
    key_base, key_row, key_col = jax.random.split(jax.random.fold_in(key, 11), 3)
    full_shape = (GRIDS, GRID, GRID, D)
    base_values = jnp.clip(jax.random.normal(key_base, full_shape, jnp.float32), -5.0, 5.0)
    row_scale = jnp.exp(jax.random.uniform(key_row, (GRIDS, GRID, GRID, 1), jnp.float32, math.log(0.3), math.log(3.0)))
    col_scale = jnp.exp(jax.random.uniform(key_col, (1, 1, 1, D), jnp.float32, math.log(0.5), math.log(2.0)))
    return (base_values * row_scale * col_scale).astype(jnp.bfloat16)


def draw_routing(key, part):
    n_devices = GRIDS * GRID * GRID // TOK_DEV
    rows_local = TOK_DEV // (GRIDS * GRID)
    group_size = EXPERTS // TOPK

    def one_block(block_key):
        sub_keys = jax.random.split(block_key, TOPK + 1)
        expert_order = jax.random.permutation(sub_keys[0], EXPERTS).astype(jnp.int32)
        columns = []
        for position in range(TOPK):
            token_ranks = jax.random.permutation(sub_keys[position + 1], TOK_DEV).astype(jnp.int32)
            columns.append(expert_order[position * group_size + token_ranks % group_size])
        return jnp.stack(columns, axis=1)
    all_blocks = jax.vmap(one_block)(jax.random.split(jax.random.fold_in(key, 7), n_devices))
    all_blocks = all_blocks.reshape(n_devices, GRIDS, rows_local, GRID, TOPK).transpose(1, 0, 2, 3, 4)
    return all_blocks.reshape(GRIDS, GRID, GRID, TOPK).astype(jnp.int32)


def shard_levels(rng, extent, shards, low, top_value):
    level = 1.0
    for dim, blocks in shards:
        heights = jax.random.uniform(jax.random.fold_in(jax.random.fold_in(rng, 6), dim), (blocks,), jnp.float32, low / len(shards), top_value / len(shards))
        level = level * jnp.repeat(jnp.exp(heights), extent[dim] // blocks).reshape((-1,) + (1,) * (len(extent) - 1 - dim))
    return level


def bell_draw(own_key, shape, scale, bound, pieces=(), held_as=jnp.bfloat16):
    result = jax.random.normal(own_key, shape, jnp.float32) * scale
    if len(pieces) > 0:
        result = shard_levels(own_key, shape, pieces, -0.22, 0.18) * result
    return jnp.clip(result, min=-bound, max=bound).astype(held_as)


def setup_inputs(seed: int = 0, part: int = 0) -> dict:
    keys = jax.random.split(jax.random.key(seed), 11)
    part_keys = jax.random.split(jax.random.fold_in(keys[10], part), 11)
    return {
        "tokens": draw_tokens(jax.random.fold_in(jax.random.fold_in(keys[10], part), 71), part),
        "ln_first": jnp.clip(1.0 + 0.1 * jax.random.normal(keys[1], (D,), jnp.float32), 0.5, 1.5),
        "spec_first": bell_draw(keys[2], (2, NB, D // NB, D // NB), (2 * D // NB) ** -0.5, 0.375),
        "spec_second": bell_draw(keys[3], (2, NB, D // NB, D // NB), (2 * D // NB) ** -0.5, 0.375),
        "spec_bias": bell_draw(keys[4], (2, D), 0.5, 3.0, (), jnp.float32),
        "ln_second": jnp.clip(1.0 + 0.1 * jax.random.normal(keys[5], (D,), jnp.float32), 0.5, 1.5),
        "routing": draw_routing(jax.random.fold_in(jax.random.fold_in(keys[10], part), 71), part),
        "combine": jnp.clip(0.1 + 0.5 * jax.random.uniform(part_keys[7], (GRIDS, GRID, GRID, TOPK), jnp.float32) ** shard_levels(part_keys[7], (GRIDS, GRID, GRID, TOPK), ((1, 16),), -0.2, 0.2), 0.1, 0.6),
        "up_weight": bell_draw(keys[8], (2 * EXPERTS, D, FF // 2), D ** -0.5, 0.1875, ((0, 8),)),
        "down_weight": bell_draw(keys[9], (2 * EXPERTS, FF // 2, D), FF ** -0.5, 0.109375, ((0, 8),)),
    }


def twiddle(length):
    counter = jnp.arange(length, dtype=jnp.float32)
    angle = 2.0 * math.pi / length * jnp.mod(jnp.outer(counter, counter), float(length))
    return (jnp.cos(angle), jnp.sin(angle))

def layer_norm(values, gain):
    values = values.astype(jnp.float32)
    center = values - lax.optimization_barrier(jnp.mean(values, axis=-1, keepdims=True))
    spread = lax.optimization_barrier(jnp.mean(center * center, axis=-1, keepdims=True))
    return center * lax.rsqrt(spread + 1e-05) * gain

def product(left, right, form):
    return jnp.einsum(form, left.astype(jnp.float32), right.astype(jnp.float32), precision=lax.Precision.HIGHEST)

def complex_blocks(real_in, imag_in, weight):
    form = 'ghkbi,bio->ghkbo'
    real_out = product(real_in, weight[0], form) - product(imag_in, weight[1], form)
    imag_out = product(real_in, weight[1], form) + product(imag_in, weight[0], form)
    return (real_out, imag_out)

def block_mlp(modes, first, second, bias):
    dims = modes.shape
    nblocks = first.shape[1]
    bwidth = first.shape[2]
    real_part = modes[:, 0].reshape(dims[0], dims[2], dims[3], nblocks, bwidth)
    imag_part = modes[:, 1].reshape(dims[0], dims[2], dims[3], nblocks, bwidth)
    hid_real, hid_imag = complex_blocks(real_part, imag_part, first)
    hid_real = jax.nn.relu(hid_real + bias[0].reshape(nblocks, bwidth)).astype(jnp.bfloat16)
    hid_imag = jax.nn.relu(hid_imag + bias[1].reshape(nblocks, bwidth)).astype(jnp.bfloat16)
    out_real, out_imag = complex_blocks(hid_real, hid_imag, second)
    return jnp.stack([out_real, out_imag], axis=1).reshape(dims).astype(jnp.bfloat16)

def reference(tokens, ln_first, spec_first, spec_second, spec_bias, ln_second, routing, combine, up_weight, down_weight):
    cosine, sine = twiddle(GRID)
    forward_cols = jnp.stack([cosine, -sine], axis=1).astype(jnp.bfloat16)
    forward_rows = jnp.stack([jnp.stack([cosine, sine], axis=1), jnp.stack([-sine, cosine], axis=1)], axis=0).astype(jnp.bfloat16)
    inverse_rows = jnp.stack([jnp.stack([cosine, -sine], axis=1), jnp.stack([sine, cosine], axis=1)], axis=0).astype(jnp.bfloat16)
    inverse_cols = jnp.stack([cosine, -sine], axis=0).astype(jnp.bfloat16)
    normed_first = layer_norm(tokens, ln_first).astype(jnp.bfloat16)
    col_spec = product(normed_first, forward_cols, 'ghwd,wck->gchkd').astype(jnp.bfloat16)
    modes = (product(forward_rows, col_spec, 'amch,gchkd->gamkd') * (1.0 / GRID)).astype(jnp.bfloat16)
    mixed_modes = block_mlp(modes, spec_first, spec_second, spec_bias)
    row_back = product(inverse_rows, mixed_modes, 'amch,gchkd->gamkd').astype(jnp.bfloat16)
    mixing = product(row_back, inverse_cols, 'gchkd,ckw->ghwd') * (1.0 / GRID)
    residual = (tokens.astype(jnp.float32) + mixing).astype(jnp.bfloat16)
    normed = layer_norm(residual, ln_second).astype(jnp.bfloat16).reshape(-1, D)
    flat_route = routing.reshape(-1).astype(jnp.int32)
    weights_flat = combine.reshape(-1)
    order_all = jnp.argsort(flat_route, stable=True).astype(jnp.int32).reshape(EXPERTS, -1)
    up_full = up_weight.reshape(EXPERTS, 2, D, FF // 2).transpose(0, 2, 1, 3).reshape(EXPERTS, D, FF)
    down_full = down_weight.reshape(EXPERTS, FF, D)

    def one_expert(inputs):
        picks, w_up, w_down = inputs
        rows_in = normed[picks // TOPK]
        hidden = jax.nn.gelu(jnp.dot(rows_in, w_up, preferred_element_type=jnp.float32), approximate=True).astype(jnp.bfloat16)
        return jnp.dot(hidden, w_down, preferred_element_type=jnp.float32) * weights_flat[picks][:, None]
    outputs = lax.map(one_expert, (order_all, up_full, down_full))
    total = jnp.zeros(normed.shape, jnp.float32).at[order_all.reshape(-1) // TOPK].add(outputs.reshape(-1, D))
    return (residual.astype(jnp.float32) + total.reshape(residual.shape)).astype(jnp.bfloat16)
```

```python
import functools
import math

import jax
import jax.numpy as jnp
import ml_dtypes
import numpy as np
from jax import lax
from jax.experimental import pallas as pl
from jax.experimental.pallas import tpu as pltpu
from jax.sharding import PartitionSpec as P

MIB = 1 << 20


def exchange(value, axis, mask):
    pairs = [(source, source ^ mask) for source in range(lax.axis_size(axis))]
    return lax.ppermute(value, axis, pairs)


def mxu(left, right):
    return jnp.dot(left, right, preferred_element_type=jnp.float32)


def normalize(values, gain):
    center = values - jnp.mean(values, axis=-1, keepdims=True)
    spread = jnp.mean(center * center, axis=-1, keepdims=True)
    return center * lax.rsqrt(spread + 1e-05) * gain


def trig(grid_len):
    counter = np.arange(grid_len)
    angle = 2.0 * math.pi / grid_len * (np.outer(counter, counter) % grid_len)
    cosine = np.round(np.cos(angle), 12).astype(ml_dtypes.bfloat16).astype(np.float64)
    sine = np.round(np.sin(angle), 12).astype(ml_dtypes.bfloat16).astype(np.float64)
    return cosine, sine


def column_tables(grid_len, n_dev, rows_local):
    cosine, sine = trig(grid_len)
    packed = grid_len // 2
    per_dev = packed // n_dev
    part = np.stack([cosine[:packed], -sine[:packed]], axis=1)
    part[0, 1] = cosine[packed]
    part = part.reshape(n_dev, per_dev, 2, grid_len)
    forward = np.zeros((per_dev, n_dev, rows_local, 2, rows_local, grid_len))
    for row in range(rows_local):
        forward[:, :, row, :, row, :] = part.transpose(1, 0, 2, 3)
    forward = forward.reshape(per_dev, n_dev * rows_local * 2, rows_local * grid_len)
    inverse = forward.transpose(0, 2, 1) / grid_len
    return forward.astype(ml_dtypes.bfloat16), inverse.astype(ml_dtypes.bfloat16)


def row_tables(grid_len):
    c, s = trig(grid_len)
    z = np.zeros_like(c)

    def assemble(blocks):
        array = np.array(blocks)
        return array.transpose(0, 1, 3, 4, 2).reshape(4 * grid_len, 2 * grid_len)

    plain_fwd = assemble([[[c, s], [-s, c]], [[c, -s], [-s, -c]]]) / grid_len
    first_fwd = assemble([[[c, z], [-s, z]], [[z, c], [z, -s]]]) / grid_len
    plain_inv = assemble([[[c, s], [-s, c]], [[c, -s], [-s, -c]]]).T
    first_inv = assemble([[[c, z], [-s, z]], [[z, c], [z, -s]]]).T
    kinds = lambda first, plain: np.stack([first, plain]).astype(ml_dtypes.bfloat16)
    return kinds(first_fwd, plain_fwd), kinds(first_inv, plain_inv)


def spectra_kernel(tokens, gain, table, out, normed):
    tile = 128
    width = tokens.shape[1]

    def norm_tile(index, carry):
        rows = pl.ds(pl.multiple_of(index * tile, tile), tile)
        values = tokens[rows, :].astype(jnp.float32)
        normed[rows, :] = normalize(values, gain[...]).astype(normed.dtype)
        return carry

    lax.fori_loop(0, tokens.shape[0] // tile, norm_tile, 0)
    for column in range(table.shape[0]):
        out[:, column * width : (column + 1) * width] = mxu(table[column], normed[...]).astype(out.dtype)


def column_spectra(tokens, gain, table):
    per_dev, rows_out, rows_in = table.shape
    width = tokens.shape[1]
    return pl.pallas_call(
        spectra_kernel,
        out_shape=jax.ShapeDtypeStruct((rows_out, per_dev * width), jnp.bfloat16),
        in_specs=[pl.BlockSpec(memory_space=pltpu.VMEM)] * 3,
        out_specs=pl.BlockSpec(memory_space=pltpu.VMEM),
        scratch_shapes=[pltpu.VMEM((rows_in, width), jnp.bfloat16)],
        compiler_params=pltpu.CompilerParams(vmem_limit_bytes=32 * MIB),
        cost_estimate=pl.CostEstimate(
            flops=2 * per_dev * rows_out * rows_in * width,
            bytes_accessed=2 * (rows_in * width + rows_out * per_dev * width + table.size),
            transcendentals=0,
        ),
        name="column_spectra",
    )(tokens, gain, table)


def modes_kernel(spectra, forward, first, second, bias, inverse, out, mixed):
    n_blocks, pair, _ = first.shape
    block = pair // 2
    grid_len = spectra.shape[0] // 2
    modes = mxu(forward[0], spectra[...]).astype(jnp.bfloat16)
    for index in range(n_blocks):
        lanes = slice(index * block, (index + 1) * block)
        sides = [
            jnp.concatenate(
                [
                    modes[2 * sign * grid_len : (2 * sign + 1) * grid_len, lanes],
                    modes[(2 * sign + 1) * grid_len : (2 * sign + 2) * grid_len, lanes],
                ],
                axis=1,
            )
            for sign in range(2)
        ]
        hid = mxu(jnp.concatenate(sides, axis=0), first[index])
        hid = jnp.maximum(hid + bias[index : index + 1, :], 0.0).astype(jnp.bfloat16)
        result = mxu(hid, second[index]).astype(jnp.bfloat16)
        for sign in range(2):
            for part in range(2):
                base = (2 * sign + part) * grid_len
                mixed[base : base + grid_len, lanes] = result[
                    sign * grid_len : (sign + 1) * grid_len, part * block : (part + 1) * block
                ]
    out[...] = mxu(inverse[0], mixed[...]).astype(out.dtype)


def mix_modes(spectra, forward, first, second, bias, inverse, width):
    rows, lanes = spectra.shape
    per_dev = lanes // width
    modes_rows = forward.shape[1]
    kind = lambda k: (jnp.minimum(k, 1), 0, 0)
    whole3 = lambda k: (0, 0, 0)
    return pl.pallas_call(
        modes_kernel,
        grid=(per_dev,),
        out_shape=jax.ShapeDtypeStruct((rows, lanes), jnp.bfloat16),
        in_specs=[
            pl.BlockSpec((rows, width), lambda k: (0, k)),
            pl.BlockSpec((1,) + forward.shape[1:], kind),
            pl.BlockSpec(first.shape, whole3),
            pl.BlockSpec(second.shape, whole3),
            pl.BlockSpec(bias.shape, lambda k: (0, 0)),
            pl.BlockSpec((1,) + inverse.shape[1:], kind),
        ],
        out_specs=pl.BlockSpec((rows, width), lambda k: (0, k)),
        scratch_shapes=[pltpu.VMEM((modes_rows, width), jnp.bfloat16)],
        compiler_params=pltpu.CompilerParams(vmem_limit_bytes=32 * MIB),
        cost_estimate=pl.CostEstimate(
            flops=2 * lanes * (2 * rows * modes_rows + modes_rows * 512),
            bytes_accessed=4 * (rows * lanes + first.size),
            transcendentals=0,
        ),
        name="mix_modes",
    )(spectra, forward, first, second, bias, inverse)


def residual_kernel(spectra, table, tokens, gain, residual, normed):
    width = tokens.shape[1]
    total = tokens[...].astype(jnp.float32)
    mixing = None
    for column in range(table.shape[0]):
        term = mxu(table[column], spectra[:, column * width : (column + 1) * width])
        mixing = term if mixing is None else mixing + term
    rounded = (total + mixing).astype(jnp.bfloat16)
    residual[...] = rounded
    normed[...] = normalize(rounded.astype(jnp.float32), gain[...]).astype(jnp.bfloat16)


def add_mixing(spectra, table, tokens, gain):
    per_dev, rows_out, rows_in = table.shape
    width = tokens.shape[1]
    tile = math.gcd(rows_out, 256)
    out = jax.ShapeDtypeStruct((rows_out, width), jnp.bfloat16)
    row_tile = pl.BlockSpec((tile, width), lambda i: (i, 0))
    return pl.pallas_call(
        residual_kernel,
        grid=(rows_out // tile,),
        out_shape=(out, out),
        in_specs=[
            pl.BlockSpec(spectra.shape, lambda i: (0, 0)),
            pl.BlockSpec((per_dev, tile, rows_in), lambda i: (0, i, 0)),
            row_tile,
            pl.BlockSpec(gain.shape, lambda i: (0, 0)),
        ],
        out_specs=(row_tile, row_tile),
        compiler_params=pltpu.CompilerParams(vmem_limit_bytes=32 * MIB),
        cost_estimate=pl.CostEstimate(
            flops=2 * per_dev * rows_out * rows_in * width,
            bytes_accessed=2 * (3 * rows_out * width + spectra.size + table.size),
            transcendentals=0,
        ),
        name="add_mixing",
    )(spectra, table, tokens, gain)


def experts_kernel(n_blocks, n_parts, tile, chunk, normed, weights, *refs):
    per_block = [1] + [n_parts] * (n_blocks - 1)
    n_pieces = sum(per_block)
    ups, downs = refs[:n_pieces], refs[n_pieces : 2 * n_pieces]
    out, up_all, down_all, up_sem, down_sem = refs[2 * n_pieces :]
    hidden = up_all.shape[2]
    copies = []
    piece = 0
    for block, parts in enumerate(per_block):
        size = hidden // parts
        for part in range(parts):
            units = pl.ds(part * size, size)
            copies.append(
                (
                    block,
                    pltpu.make_async_copy(ups[piece], up_all.at[block, :, units], up_sem.at[piece]),
                    pltpu.make_async_copy(downs[piece], down_all.at[block, units, :], down_sem.at[piece]),
                )
            )
            piece += 1
    for _, up_copy, down_copy in copies:
        up_copy.start()
        down_copy.start()
    for block in range(n_blocks):
        for owner, up_copy, down_copy in copies:
            if owner == block:
                up_copy.wait()
                down_copy.wait()

        def token_tile(index, carry, block=block):
            rows = pl.ds(pl.multiple_of(index * tile, tile), tile)
            values = normed[rows, :]
            total = None
            for start in range(0, hidden, chunk):
                units = slice(start, start + chunk)
                act = jax.nn.gelu(mxu(values, up_all[block, :, units]), approximate=True)
                term = mxu(act.astype(jnp.bfloat16), down_all[block, units, :])
                total = term if total is None else total + term
            column = block // 2
            total = total * weights[rows, column : column + 1]
            if block > 0:
                total = total + out[rows, :]
            out[rows, :] = total
            return carry

        lax.fori_loop(0, normed.shape[0] // tile, token_tile, 0)


def run_experts(normed, weights, blocks, tile=256, chunk=512):
    rows, width = normed.shape
    ups = [up for block in blocks for up, _ in block]
    downs = [down for block in blocks for _, down in block]
    n_blocks = len(blocks)
    hidden = blocks[0][0][0].shape[1]
    chunk = math.gcd(chunk, hidden)
    n_parts = len(blocks[-1])
    vmem = pl.BlockSpec(memory_space=pltpu.VMEM)
    return pl.pallas_call(
        functools.partial(experts_kernel, n_blocks, n_parts, tile, chunk),
        out_shape=jax.ShapeDtypeStruct((rows, width), jnp.float32),
        in_specs=[vmem, vmem] + [pl.BlockSpec(memory_space=pl.ANY)] * (2 * len(ups)),
        out_specs=vmem,
        scratch_shapes=[
            pltpu.VMEM((n_blocks, width, hidden), jnp.bfloat16),
            pltpu.VMEM((n_blocks, hidden, width), jnp.bfloat16),
            pltpu.SemaphoreType.DMA((len(ups),)),
            pltpu.SemaphoreType.DMA((len(ups),)),
        ],
        compiler_params=pltpu.CompilerParams(vmem_limit_bytes=56 * MIB),
        cost_estimate=pl.CostEstimate(
            flops=4 * rows * width * hidden * n_blocks,
            bytes_accessed=4 * width * hidden * n_blocks + 8 * rows * width,
            transcendentals=rows * hidden * n_blocks,
        ),
        name="experts",
    )(normed, weights, *ups, *downs)


def expert_weights(routing, combine, experts):
    return jnp.stack(
        [jnp.sum(jnp.where(routing == expert, combine, 0.0), axis=-1) for expert in experts], axis=-1
    )


def gather_blocks(up, down):
    n_parts = lax.axis_size("group") * lax.axis_size("expert")
    part = lax.axis_index("group") * lax.axis_size("expert") + lax.axis_index("expert")
    size = up.shape[1] // n_parts
    mine = (
        lax.dynamic_slice_in_dim(up, part * size, size, axis=1),
        lax.dynamic_slice_in_dim(down, part * size, size, axis=0),
    )
    far = exchange(mine, "row", 4)
    near = exchange(mine, "row", 1)
    far_near = exchange(far, "row", 1)
    blocks = [[(up, down)]]
    for piece in (near, far, far_near):
        other = exchange(piece, "group", 1)
        blocks.append([piece, other, exchange(piece, "expert", 1), exchange(other, "expert", 1)])
    return blocks


def all_experts(residual, normed, routing, combine, up_weight, down_weight):
    mine = lax.axis_index("row") // 2
    flat = lambda value: value.reshape(-1, value.shape[-1])
    weights = lambda first: expert_weights(flat(routing), flat(combine), (first, first ^ 2))
    other_weights = exchange(weights(mine ^ 1).T, "row", 2).T
    blocks = gather_blocks(up_weight[0], down_weight[0])
    other = exchange(normed, "row", 2)
    own_out = run_experts(normed, weights(mine), blocks)
    other_out = run_experts(other, other_weights, blocks).astype(jnp.bfloat16)
    returned = exchange(other_out, "row", 2)
    return residual.astype(jnp.float32) + own_out + returned.astype(jnp.float32)


def routed_experts(residual, normed, routing, combine, up_weight, down_weight):
    n_tokens, width = normed.shape
    top_count = routing.shape[-1]
    experts = lax.axis_size("row") // 2
    capacity = n_tokens * top_count // experts
    flat_route = routing.reshape(-1)
    one_hot = (flat_route[:, None] == jnp.arange(experts, dtype=jnp.int32)[None, :]).astype(jnp.int32)
    earlier = jnp.cumsum(one_hot, axis=0) - one_hot
    slot_index = flat_route * capacity + jnp.sum(earlier * one_hot, axis=1)
    token_of = jnp.arange(n_tokens * top_count, dtype=jnp.int32) // top_count
    source_row = jnp.zeros((experts * capacity,), jnp.int32).at[slot_index].set(token_of)
    send_rows = normed[source_row].reshape(experts, capacity, width)
    partner_up, partner_down = exchange((up_weight, down_weight), "row", 1)
    up_full = jnp.concatenate([up_weight[0], partner_up[0]], axis=1)
    down_full = jnp.concatenate([down_weight[0], partner_down[0]], axis=0)
    outgoing = send_rows.reshape(experts * 2, capacity // 2, width)
    arrived = lax.all_to_all(outgoing, "row", split_axis=0, concat_axis=0, tiled=True)
    hidden = jax.nn.gelu(mxu(arrived.reshape(-1, width), up_full), approximate=True).astype(jnp.bfloat16)
    partial_out = mxu(hidden, down_full).reshape(arrived.shape).astype(jnp.bfloat16)
    returned = lax.all_to_all(partial_out, "row", split_axis=0, concat_axis=0, tiled=True)
    gathered = returned.reshape(-1, width)[slot_index].reshape(n_tokens, top_count, width)
    scaled = gathered.astype(jnp.float32) * combine.reshape(n_tokens, top_count, 1)
    return residual.astype(jnp.float32) + jnp.sum(scaled, axis=1)


def complex_weight(weight):
    real, imag = weight[0], weight[1]
    return jnp.concatenate(
        [jnp.concatenate([real, imag], axis=2), jnp.concatenate([-imag, real], axis=2)], axis=1
    )


def per_device(
    tokens,
    ln_first,
    spec_first,
    spec_second,
    spec_bias,
    ln_second,
    routing,
    combine,
    up_weight,
    down_weight,
):
    _, rows_local, grid_len, width = tokens.shape
    axes = ("row", "expert")
    n_dev = lax.axis_size(axes)
    n_blocks = spec_first.shape[1]
    forward_cols, inverse_cols = column_tables(grid_len, n_dev, rows_local)
    forward_rows, inverse_rows = row_tables(grid_len)
    first_device = lax.axis_index(axes) == 0
    pick = lambda table: jnp.stack([jnp.where(first_device, table[0], table[1]), table[1]])
    flat_tokens = tokens.reshape(-1, width)

    spectra = column_spectra(flat_tokens, ln_first.reshape(1, width), jnp.asarray(forward_cols))
    by_column = lax.all_to_all(
        spectra.reshape(n_dev, -1, spectra.shape[1]), axes, split_axis=0, concat_axis=0, tiled=True
    )
    bias = spec_bias.reshape(2, n_blocks, -1).transpose(1, 0, 2).reshape(n_blocks, -1)
    mixed = mix_modes(
        by_column.reshape(spectra.shape),
        pick(forward_rows),
        complex_weight(spec_first),
        complex_weight(spec_second),
        bias,
        pick(inverse_rows),
        width,
    )
    by_row = lax.all_to_all(
        mixed.reshape(n_dev, -1, mixed.shape[1]), axes, split_axis=0, concat_axis=0, tiled=True
    )
    residual, normed = add_mixing(
        by_row.reshape(mixed.shape), jnp.asarray(inverse_cols), flat_tokens, ln_second.reshape(1, width)
    )
    pairs = lax.axis_size("group") == 2 and lax.axis_size("expert") == 2
    every_expert = lax.axis_size("row") == 2 * routing.shape[-1] and routing.shape[-1] == 4
    moe = all_experts if pairs and every_expert else routed_experts
    final = moe(residual, normed, routing, combine, up_weight, down_weight)
    return final.astype(jnp.bfloat16).reshape(tokens.shape)


def solution(mesh):
    placed = (
        P("group", ("row", "expert"), None, None),
        P(),
        P(),
        P(),
        P(),
        P(),
        P("group", ("row", "expert"), None, None),
        P("group", ("row", "expert"), None, None),
        P("row", None, None),
        P("row", None, None),
    )
    return jax.shard_map(
        per_device,
        mesh=mesh,
        in_specs=placed,
        out_specs=P("group", ("row", "expert"), None, None),
        check_vma=False,
    )
```

```python
import functools
import math

import jax
import jax.numpy as jnp
import ml_dtypes
import numpy as np
from jax import lax
from jax.experimental import pallas as pl
from jax.experimental.pallas import tpu as pltpu
from jax.sharding import PartitionSpec as P

MIB = 1 << 20


def exchange(value, axis, mask):
    pairs = [(source, source ^ mask) for source in range(lax.axis_size(axis))]
    return lax.ppermute(value, axis, pairs)


def mxu(left, right):
    return jnp.dot(left, right, preferred_element_type=jnp.float32)


def normalize(values, gain):
    center = values - jnp.mean(values, axis=-1, keepdims=True)
    spread = jnp.mean(center * center, axis=-1, keepdims=True)
    return center * lax.rsqrt(spread + 1e-05) * gain


def trig(grid_len):
    counter = np.arange(grid_len)
    angle = 2.0 * math.pi / grid_len * (np.outer(counter, counter) % grid_len)
    cosine = np.round(np.cos(angle), 12).astype(ml_dtypes.bfloat16).astype(np.float64)
    sine = np.round(np.sin(angle), 12).astype(ml_dtypes.bfloat16).astype(np.float64)
    return cosine, sine


def column_tables(grid_len, n_dev, rows_local):
    cosine, sine = trig(grid_len)
    packed = grid_len // 2
    per_dev = packed // n_dev
    part = np.stack([cosine[:packed], -sine[:packed]], axis=1)
    part[0, 1] = cosine[packed]
    part = part.reshape(n_dev, per_dev, 2, grid_len)
    forward = np.zeros((per_dev, n_dev, rows_local, 2, rows_local, grid_len))
    for row in range(rows_local):
        forward[:, :, row, :, row, :] = part.transpose(1, 0, 2, 3)
    forward = forward.reshape(per_dev, n_dev * rows_local * 2, rows_local * grid_len)
    inverse = forward.transpose(0, 2, 1) / grid_len
    return forward.astype(ml_dtypes.bfloat16), inverse.astype(ml_dtypes.bfloat16)


def row_tables(grid_len, rows_local, n_halves):
    c, s = trig(grid_len)
    z = np.zeros_like(c)

    def assemble(blocks):
        array = np.array(blocks)
        return array.transpose(0, 1, 3, 4, 2).reshape(4 * grid_len, 2 * grid_len)

    plain_fwd = assemble([[[c, s], [-s, c]], [[c, -s], [-s, -c]]]) / grid_len
    first_fwd = assemble([[[c, z], [-s, z]], [[z, c], [z, -s]]]) / grid_len
    plain_inv = assemble([[[c, s], [-s, c]], [[c, -s], [-s, -c]]]).T
    first_inv = assemble([[[c, z], [-s, z]], [[z, c], [z, -s]]]).T
    kinds = lambda first, plain: np.stack([first, plain]).astype(ml_dtypes.bfloat16)
    inverse = kinds(first_inv, plain_inv)
    inverse = inverse.reshape(2, -1, n_halves, 2 * rows_local // n_halves, 4 * grid_len).transpose(0, 2, 1, 3, 4)
    return kinds(first_fwd, plain_fwd), inverse.reshape(2, 2 * grid_len, 4 * grid_len)


def spectra_kernel(tokens, gain, table, out, normed):
    tile = 128
    width = tokens.shape[1]

    def norm_tile(index, carry):
        rows = pl.ds(pl.multiple_of(index * tile, tile), tile)
        values = tokens[rows, :].astype(jnp.float32)
        normed[rows, :] = normalize(values, gain[...]).astype(normed.dtype)
        return carry

    lax.fori_loop(0, tokens.shape[0] // tile, norm_tile, 0)
    for column in range(table.shape[0]):
        out[:, column * width : (column + 1) * width] = mxu(table[column], normed[...]).astype(out.dtype)


def column_spectra(tokens, gain, table):
    per_dev, rows_out, rows_in = table.shape
    width = tokens.shape[1]
    return pl.pallas_call(
        spectra_kernel,
        out_shape=jax.ShapeDtypeStruct((rows_out, per_dev * width), jnp.bfloat16),
        in_specs=[pl.BlockSpec(memory_space=pltpu.VMEM)] * 3,
        out_specs=pl.BlockSpec(memory_space=pltpu.VMEM),
        scratch_shapes=[pltpu.VMEM((rows_in, width), jnp.bfloat16)],
        compiler_params=pltpu.CompilerParams(vmem_limit_bytes=32 * MIB),
        cost_estimate=pl.CostEstimate(
            flops=2 * per_dev * rows_out * rows_in * width,
            bytes_accessed=2 * (rows_in * width + rows_out * per_dev * width + table.size),
            transcendentals=0,
        ),
        name="column_spectra",
    )(tokens, gain, table)


def modes_kernel(spectra, forward, first, second, bias, inverse, *refs):
    outs, mixed = refs[:-1], refs[-1]
    n_blocks, pair, _ = first.shape
    block = pair // 2
    grid_len = spectra.shape[0] // 2
    modes = mxu(forward[0], spectra[...]).astype(jnp.bfloat16)
    for index in range(n_blocks):
        lanes = slice(index * block, (index + 1) * block)
        sides = [
            jnp.concatenate(
                [
                    modes[2 * sign * grid_len : (2 * sign + 1) * grid_len, lanes],
                    modes[(2 * sign + 1) * grid_len : (2 * sign + 2) * grid_len, lanes],
                ],
                axis=1,
            )
            for sign in range(2)
        ]
        hid = mxu(jnp.concatenate(sides, axis=0), first[index])
        hid = jnp.maximum(hid + bias[index : index + 1, :], 0.0).astype(jnp.bfloat16)
        result = mxu(hid, second[index]).astype(jnp.bfloat16)
        for sign in range(2):
            for part in range(2):
                base = (2 * sign + part) * grid_len
                mixed[base : base + grid_len, lanes] = result[
                    sign * grid_len : (sign + 1) * grid_len, part * block : (part + 1) * block
                ]
    back = mxu(inverse[0], mixed[...]).astype(jnp.bfloat16)
    rows = outs[0].shape[0]
    for index, out in enumerate(outs):
        out[...] = back[index * rows : (index + 1) * rows, :]


def mix_modes(spectra, forward, first, second, bias, inverse, width, n_halves):
    rows, lanes = spectra.shape
    rows_out = rows // n_halves
    per_dev = lanes // width
    modes_rows = forward.shape[1]
    kind = lambda k: (jnp.minimum(k, 1), 0, 0)
    whole3 = lambda k: (0, 0, 0)
    return pl.pallas_call(
        modes_kernel,
        grid=(per_dev,),
        out_shape=[jax.ShapeDtypeStruct((rows_out, lanes), jnp.bfloat16)] * n_halves,
        in_specs=[
            pl.BlockSpec((rows, width), lambda k: (0, k)),
            pl.BlockSpec((1,) + forward.shape[1:], kind),
            pl.BlockSpec(first.shape, whole3),
            pl.BlockSpec(second.shape, whole3),
            pl.BlockSpec(bias.shape, lambda k: (0, 0)),
            pl.BlockSpec((1,) + inverse.shape[1:], kind),
        ],
        out_specs=[pl.BlockSpec((rows_out, width), lambda k: (0, k))] * n_halves,
        scratch_shapes=[pltpu.VMEM((modes_rows, width), jnp.bfloat16)],
        compiler_params=pltpu.CompilerParams(vmem_limit_bytes=32 * MIB),
        cost_estimate=pl.CostEstimate(
            flops=2 * lanes * (2 * rows * modes_rows + modes_rows * 512),
            bytes_accessed=4 * (rows * lanes + first.size),
            transcendentals=0,
        ),
        name="mix_modes",
    )(spectra, forward, first, second, bias, inverse)


def residual_kernel(spectra, table, tokens, gain, residual, normed):
    width = tokens.shape[1]
    total = tokens[...].astype(jnp.float32)
    mixing = None
    for column in range(table.shape[0]):
        term = mxu(table[column], spectra[:, column * width : (column + 1) * width])
        mixing = term if mixing is None else mixing + term
    rounded = (total + mixing).astype(jnp.bfloat16)
    residual[...] = rounded
    normed[...] = normalize(rounded.astype(jnp.float32), gain[...]).astype(jnp.bfloat16)


def add_mixing(spectra, table, tokens, gain, half):
    per_dev, rows_out, rows_in = table.shape
    width = tokens.shape[1]
    tile = math.gcd(rows_out, 256)
    out = jax.ShapeDtypeStruct((rows_out, width), jnp.bfloat16)
    row_tile = pl.BlockSpec((tile, width), lambda i: (i, 0))
    base = half * (rows_out // tile)
    return pl.pallas_call(
        residual_kernel,
        grid=(rows_out // tile,),
        out_shape=(out, out),
        in_specs=[
            pl.BlockSpec(spectra.shape, lambda i: (0, 0)),
            pl.BlockSpec((per_dev, tile, rows_in), lambda i: (0, i, 0)),
            pl.BlockSpec((tile, width), lambda i: (i + base, 0)),
            pl.BlockSpec(gain.shape, lambda i: (0, 0)),
        ],
        out_specs=(row_tile, row_tile),
        compiler_params=pltpu.CompilerParams(vmem_limit_bytes=32 * MIB),
        cost_estimate=pl.CostEstimate(
            flops=2 * per_dev * rows_out * rows_in * width,
            bytes_accessed=2 * (3 * rows_out * width + spectra.size + table.size),
            transcendentals=0,
        ),
        name="add_mixing",
    )(spectra, table, tokens, gain)


def gelu_twice(values):
    scale = math.sqrt(2.0 / math.pi)
    return values * jnp.tanh(values * (values * values * (0.044715 * scale) + scale)) + values


def experts_kernel(pieces, n_sets, n_totals, chunk, weights, *refs):
    n_pieces = sum(pieces)
    take = iter(refs)
    sets = [next(take) for _ in range(n_sets)]
    totals = [next(take) for _ in range(n_totals)]
    ups = [next(take) for _ in range(n_pieces)]
    downs = [next(take) for _ in range(n_pieces)]
    outs = [next(take) for _ in range(n_sets)]
    values, total, up_all, down_all, set_sem, total_sem, up_sem, down_sem = take
    n_blocks, _, hidden = up_all.shape
    tile = values.shape[0] // n_sets
    loads = []
    for index, ref in enumerate(sets):
        loads.append(pltpu.make_async_copy(ref, values.at[pl.ds(index * tile, tile)], set_sem.at[index]))
    total_loads = []
    for index, ref in enumerate(totals):
        total_loads.append(pltpu.make_async_copy(ref, total.at[pl.ds(index * tile, tile)], total_sem.at[index]))
    blocks = []
    piece = 0
    for block, parts in enumerate(pieces):
        size = hidden // parts
        copies = []
        for part in range(parts):
            units = pl.ds(part * size, size)
            copies.append(pltpu.make_async_copy(ups[piece], up_all.at[block, :, units], up_sem.at[piece]))
            copies.append(pltpu.make_async_copy(downs[piece], down_all.at[block, units, :], down_sem.at[piece]))
            piece += 1
        blocks.append(copies)
    for copy in loads + [copy for copies in blocks for copy in copies] + total_loads:
        copy.start()
    for copy in loads:
        copy.wait()

    def step(index, carry):
        block = index // n_sets
        rows = pl.ds(pl.multiple_of((index % n_sets) * tile, tile), tile)
        for number in range(n_blocks):

            @pl.when(index == number * n_sets)
            def _(number=number):
                for copy in blocks[number]:
                    copy.wait()

        if n_totals:

            @pl.when(index == 0)
            def _():
                for copy in total_loads:
                    copy.wait()

        given = values[rows, :]
        acts = [
            gelu_twice(mxu(given, up_all[block, :, start : start + chunk])).astype(jnp.bfloat16)
            for start in range(0, hidden, chunk)
        ]
        term = mxu(jnp.concatenate(acts, axis=1), down_all[block])
        scale = weights[rows, 0:1]
        for number in range(1, n_blocks):
            scale = jnp.where(block == number, weights[rows, number : number + 1], scale)
        term = term * (0.5 * scale)
        if n_totals:
            total[rows, :] = total[rows, :] + term
        else:

            @pl.when(block == 0)
            def _():
                total[rows, :] = term

            @pl.when(block > 0)
            def _():
                total[rows, :] = total[rows, :] + term

        return carry

    lax.fori_loop(0, n_blocks * n_sets, step, 0)
    for index, out in enumerate(outs):
        out[...] = total[index * tile : (index + 1) * tile, :].astype(out.dtype)


def run_experts(sets, weights, blocks, totals=(), dtype=jnp.float32, chunk=256):
    rows, width = sets[0].shape
    ups = [up for block in blocks for up, _ in block]
    downs = [down for block in blocks for _, down in block]
    pieces = tuple(len(block) for block in blocks)
    n_blocks = len(blocks)
    hidden = sum(up.shape[1] for up, _ in blocks[0])
    chunk = math.gcd(chunk, hidden)
    n_rows = rows * len(sets)
    vmem = pl.BlockSpec(memory_space=pltpu.VMEM)
    anywhere = pl.BlockSpec(memory_space=pl.ANY)
    return pl.pallas_call(
        functools.partial(experts_kernel, pieces, len(sets), len(totals), chunk),
        out_shape=[jax.ShapeDtypeStruct((rows, width), dtype)] * len(sets),
        in_specs=[vmem] + [anywhere] * (len(sets) + len(totals) + 2 * len(ups)),
        out_specs=[vmem] * len(sets),
        scratch_shapes=[
            pltpu.VMEM((n_rows, width), jnp.bfloat16),
            pltpu.VMEM((n_rows, width), jnp.float32),
            pltpu.VMEM((n_blocks, width, hidden), jnp.bfloat16),
            pltpu.VMEM((n_blocks, hidden, width), jnp.bfloat16),
            pltpu.SemaphoreType.DMA((len(sets),)),
            pltpu.SemaphoreType.DMA((max(len(totals), 1),)),
            pltpu.SemaphoreType.DMA((len(ups),)),
            pltpu.SemaphoreType.DMA((len(ups),)),
        ],
        compiler_params=pltpu.CompilerParams(vmem_limit_bytes=56 * MIB),
        cost_estimate=pl.CostEstimate(
            flops=4 * n_rows * width * hidden * n_blocks,
            bytes_accessed=4 * width * hidden * n_blocks + 8 * n_rows * width,
            transcendentals=n_rows * hidden * n_blocks,
        ),
        name="experts",
    )(weights, *sets, *totals, *ups, *downs)


def expert_weights(routing, combine, n_experts):
    route, weight = (value.reshape(-1, value.shape[-1]) for value in (routing, combine))
    return jnp.stack([jnp.sum(jnp.where(route == e, weight, 0.0), axis=-1) for e in range(n_experts)])


def after(value, *others):
    return lax.optimization_barrier((value,) + others)[0]


class Weights:
    def __init__(self, up, down):
        n_parts = lax.axis_size("group") * lax.axis_size("expert")
        part = lax.axis_index("group") * lax.axis_size("expert") + lax.axis_index("expert")
        size = up.shape[1] // n_parts
        self.own = [(up, down)]
        self.part = (
            lax.dynamic_slice_in_dim(up, part * size, size, axis=1),
            lax.dynamic_slice_in_dim(down, part * size, size, axis=0),
        )

    @staticmethod
    def spread(piece):
        other = exchange(piece, "group", 1)
        return [piece, other, exchange(piece, "expert", 1), exchange(other, "expert", 1)]


def routed_experts(residual, normed, routing, combine, up_weight, down_weight):
    n_tokens, width = normed.shape
    top_count = routing.shape[-1]
    experts = lax.axis_size("row") // 2
    capacity = n_tokens * top_count // experts
    flat_route = routing.reshape(-1)
    one_hot = (flat_route[:, None] == jnp.arange(experts, dtype=jnp.int32)[None, :]).astype(jnp.int32)
    earlier = jnp.cumsum(one_hot, axis=0) - one_hot
    slot_index = flat_route * capacity + jnp.sum(earlier * one_hot, axis=1)
    token_of = jnp.arange(n_tokens * top_count, dtype=jnp.int32) // top_count
    source_row = jnp.zeros((experts * capacity,), jnp.int32).at[slot_index].set(token_of)
    send_rows = normed[source_row].reshape(experts, capacity, width)
    partner_up, partner_down = exchange((up_weight, down_weight), "row", 1)
    up_full = jnp.concatenate([up_weight[0], partner_up[0]], axis=1)
    down_full = jnp.concatenate([down_weight[0], partner_down[0]], axis=0)
    outgoing = send_rows.reshape(experts * 2, capacity // 2, width)
    arrived = lax.all_to_all(outgoing, "row", split_axis=0, concat_axis=0, tiled=True)
    hidden = jax.nn.gelu(mxu(arrived.reshape(-1, width), up_full), approximate=True).astype(jnp.bfloat16)
    partial_out = mxu(hidden, down_full).reshape(arrived.shape).astype(jnp.bfloat16)
    returned = lax.all_to_all(partial_out, "row", split_axis=0, concat_axis=0, tiled=True)
    gathered = returned.reshape(-1, width)[slot_index].reshape(n_tokens, top_count, width)
    scaled = gathered.astype(jnp.float32) * combine.reshape(n_tokens, top_count, 1)
    return residual.astype(jnp.float32) + jnp.sum(scaled, axis=1)


def complex_weight(weight):
    real, imag = weight[0], weight[1]
    return jnp.concatenate(
        [jnp.concatenate([real, imag], axis=2), jnp.concatenate([-imag, real], axis=2)], axis=1
    )


def per_device(
    tokens,
    ln_first,
    spec_first,
    spec_second,
    spec_bias,
    ln_second,
    routing,
    combine,
    up_weight,
    down_weight,
):
    _, rows_local, grid_len, width = tokens.shape
    axes = ("row", "expert")
    n_dev = lax.axis_size(axes)
    n_blocks = spec_first.shape[1]
    n_halves = math.gcd(2, rows_local)
    forward_cols, _ = column_tables(grid_len, n_dev, rows_local)
    _, inverse_cols = column_tables(grid_len, n_dev, rows_local // n_halves)
    forward_rows, inverse_rows = row_tables(grid_len, rows_local, n_halves)
    first_device = lax.axis_index(axes) == 0
    pick = lambda table: jnp.stack([jnp.where(first_device, table[0], table[1]), table[1]])
    flat_tokens = tokens.reshape(-1, width)

    spectra = column_spectra(flat_tokens, ln_first.reshape(1, width), jnp.asarray(forward_cols))
    by_column = lax.all_to_all(
        spectra.reshape(n_dev, -1, spectra.shape[1]), axes, split_axis=0, concat_axis=0, tiled=True
    )
    bias = spec_bias.reshape(2, n_blocks, -1).transpose(1, 0, 2).reshape(n_blocks, -1)
    pairs = lax.axis_size("group") == 2 and lax.axis_size("expert") == 2
    every_expert = lax.axis_size("row") == 2 * routing.shape[-1] and routing.shape[-1] == 4
    dense = pairs and every_expert and n_halves == 2
    if dense:
        weights = Weights(up_weight[0], down_weight[0])
        table = expert_weights(routing, combine, routing.shape[-1])
        arriving = (exchange(table[:, : table.shape[1] // 2], "row", 1), exchange(table[:, table.shape[1] // 2 :], "row", 2))
        near = exchange(weights.part, "row", 3)
        far_up = exchange(weights.part[0], "row", 4)
        by_column, near, far_up, arriving = lax.optimization_barrier((by_column, near, far_up, arriving))
    mixed = mix_modes(
        by_column.reshape(spectra.shape),
        pick(forward_rows),
        complex_weight(spec_first),
        complex_weight(spec_second),
        bias,
        pick(inverse_rows),
        width,
        n_halves,
    )
    by_row = [
        lax.all_to_all(half.reshape(n_dev, -1, half.shape[1]), axes, split_axis=0, concat_axis=0, tiled=True)
        for half in mixed
    ]
    if dense:
        near_all = Weights.spread(near)
        far_down = exchange(after(weights.part[1], by_column), "row", 4)
        far_near_up = exchange(far_up, "row", 3)
        by_row[0], near_all, far_down, far_near_up = lax.optimization_barrier(
            (by_row[0], near_all, far_down, far_near_up)
        )
    sides = []
    for half, spectrum in enumerate(by_row):
        sides.append(
            add_mixing(
                spectrum.reshape(mixed[0].shape),
                jnp.asarray(inverse_cols),
                flat_tokens,
                ln_second.reshape(1, width),
                half,
            )
        )
    if not dense:
        residual, normed = (jnp.concatenate(parts) for parts in zip(*sides))
        final = routed_experts(residual, normed, routing, combine, up_weight, down_weight)
        return final.astype(jnp.bfloat16).reshape(tokens.shape)

    far_near_down = exchange(far_down, "row", 3)
    far_all = Weights.spread((far_up, far_down))
    far_near_all = Weights.spread((far_near_up, far_near_down))
    expert = lax.axis_index("row") // 2
    half_size = table.shape[1] // 2
    pick_two = lambda columns, first: jnp.stack(
        [lax.dynamic_index_in_dim(columns, expert ^ (first + k), 0, keepdims=False) for k in range(2)], axis=1
    )
    (res_a, norm_a), (res_b, norm_b) = sides
    from_y = exchange(norm_a, "row", 1)
    from_z = exchange(norm_b, "row", 2)
    table_a, table_b = table[:, :half_size], table[:, half_size:]
    table_in = jnp.concatenate(arriving, axis=1)
    lower, upper = [weights.own, near_all], [far_all, far_near_all]
    own_a = run_experts([norm_a], pick_two(table_a, 0), lower)[0]
    own_b = run_experts([norm_b], pick_two(table_b, 0), lower)[0]
    others = run_experts([from_y, from_z], pick_two(table_in, 0), lower)
    back_y, back_z = run_experts([from_y, from_z], pick_two(table_in, 2), upper, others, jnp.bfloat16)
    back_a = exchange(back_y, "row", 1)
    back_b = exchange(back_z, "row", 2)
    own_a, own_b = run_experts([norm_a, norm_b], pick_two(table, 2), upper, [own_a, own_b])
    final = [
        (residual.astype(jnp.float32) + own + back.astype(jnp.float32)).astype(jnp.bfloat16)
        for residual, own, back in ((res_a, own_a, back_a), (res_b, own_b, back_b))
    ]
    return jnp.concatenate(final).reshape(tokens.shape)


def solution(mesh):
    placed = (
        P("group", ("row", "expert"), None, None),
        P(),
        P(),
        P(),
        P(),
        P(),
        P("group", ("row", "expert"), None, None),
        P("group", ("row", "expert"), None, None),
        P("row", None, None),
        P("row", None, None),
    )
    return jax.shard_map(
        per_device,
        mesh=mesh,
        in_specs=placed,
        out_specs=P("group", ("row", "expert"), None, None),
        check_vma=False,
    )
```

```python
import functools
import math

import jax
import jax.numpy as jnp
import ml_dtypes
import numpy as np
from jax import lax
from jax.experimental import pallas as pl
from jax.experimental.pallas import tpu as pltpu
from jax.sharding import PartitionSpec as P

MIB = 1 << 20


def exchange(value, axis, mask):
    pairs = [(source, source ^ mask) for source in range(lax.axis_size(axis))]
    return lax.ppermute(value, axis, pairs)


def mxu(left, right):
    return jnp.dot(left, right, preferred_element_type=jnp.float32)


def normalize(values, gain):
    center = values - jnp.mean(values, axis=-1, keepdims=True)
    spread = jnp.mean(center * center, axis=-1, keepdims=True)
    return center * lax.rsqrt(spread + 1e-05) * gain


def trig(grid_len):
    counter = np.arange(grid_len)
    angle = 2.0 * math.pi / grid_len * (np.outer(counter, counter) % grid_len)
    cosine = np.round(np.cos(angle), 12).astype(ml_dtypes.bfloat16).astype(np.float64)
    sine = np.round(np.sin(angle), 12).astype(ml_dtypes.bfloat16).astype(np.float64)
    return cosine, sine


def column_tables(grid_len, n_dev, rows_local):
    cosine, sine = trig(grid_len)
    packed = grid_len // 2
    per_dev = packed // n_dev
    part = np.stack([cosine[:packed], -sine[:packed]], axis=1)
    part[0, 1] = cosine[packed]
    part = part.reshape(n_dev, per_dev, 2, grid_len)
    forward = np.zeros((per_dev, n_dev, rows_local, 2, rows_local, grid_len))
    for row in range(rows_local):
        forward[:, :, row, :, row, :] = part.transpose(1, 0, 2, 3)
    forward = forward.reshape(per_dev, n_dev * rows_local * 2, rows_local * grid_len)
    inverse = forward.transpose(0, 2, 1) / grid_len
    return forward.astype(ml_dtypes.bfloat16), inverse.astype(ml_dtypes.bfloat16)


def row_tables(grid_len):
    c, s = trig(grid_len)
    z = np.zeros_like(c)

    def assemble(blocks):
        array = np.array(blocks)
        return array.transpose(0, 1, 3, 4, 2).reshape(4 * grid_len, 2 * grid_len)

    plain_fwd = assemble([[[c, s], [-s, c]], [[c, -s], [-s, -c]]]) / grid_len
    first_fwd = assemble([[[c, z], [-s, z]], [[z, c], [z, -s]]]) / grid_len
    plain_inv = assemble([[[c, s], [-s, c]], [[c, -s], [-s, -c]]]).T
    first_inv = assemble([[[c, z], [-s, z]], [[z, c], [z, -s]]]).T
    kinds = lambda first, plain: np.stack([first, plain]).astype(ml_dtypes.bfloat16)
    return kinds(first_fwd, plain_fwd), kinds(first_inv, plain_inv)


def spectra_kernel(tokens, gain, table, out, normed):
    tile = 128
    width = tokens.shape[1]

    def norm_tile(index, carry):
        rows = pl.ds(pl.multiple_of(index * tile, tile), tile)
        values = tokens[rows, :].astype(jnp.float32)
        normed[rows, :] = normalize(values, gain[...]).astype(normed.dtype)
        return carry

    lax.fori_loop(0, tokens.shape[0] // tile, norm_tile, 0)
    for column in range(table.shape[0]):
        out[:, column * width : (column + 1) * width] = mxu(table[column], normed[...]).astype(out.dtype)


def column_spectra(tokens, gain, table):
    per_dev, rows_out, rows_in = table.shape
    width = tokens.shape[1]
    return pl.pallas_call(
        spectra_kernel,
        out_shape=jax.ShapeDtypeStruct((rows_out, per_dev * width), jnp.bfloat16),
        in_specs=[pl.BlockSpec(memory_space=pltpu.VMEM)] * 3,
        out_specs=pl.BlockSpec(memory_space=pltpu.VMEM),
        scratch_shapes=[pltpu.VMEM((rows_in, width), jnp.bfloat16)],
        compiler_params=pltpu.CompilerParams(vmem_limit_bytes=60 * MIB),
        cost_estimate=pl.CostEstimate(
            flops=2 * per_dev * rows_out * rows_in * width,
            bytes_accessed=2 * (rows_in * width + rows_out * per_dev * width + table.size),
            transcendentals=0,
        ),
        name="column_spectra",
    )(tokens, gain, table)


def modes_kernel(spectra, forward, first, second, bias, inverse, out, mixed):
    n_blocks, pair, _ = first.shape
    block = pair // 2
    grid_len = spectra.shape[0] // 2
    modes = mxu(forward[0], spectra[...]).astype(jnp.bfloat16)
    for index in range(n_blocks):
        lanes = slice(index * block, (index + 1) * block)
        sides = [
            jnp.concatenate(
                [
                    modes[2 * sign * grid_len : (2 * sign + 1) * grid_len, lanes],
                    modes[(2 * sign + 1) * grid_len : (2 * sign + 2) * grid_len, lanes],
                ],
                axis=1,
            )
            for sign in range(2)
        ]
        hid = mxu(jnp.concatenate(sides, axis=0), first[index])
        hid = jnp.maximum(hid + bias[index : index + 1, :], 0.0).astype(jnp.bfloat16)
        result = mxu(hid, second[index]).astype(jnp.bfloat16)
        for sign in range(2):
            for part in range(2):
                base = (2 * sign + part) * grid_len
                mixed[base : base + grid_len, lanes] = result[
                    sign * grid_len : (sign + 1) * grid_len, part * block : (part + 1) * block
                ]
    out[...] = mxu(inverse[0], mixed[...]).astype(out.dtype)


def mix_modes(spectra, forward, first, second, bias, inverse, width):
    rows, lanes = spectra.shape
    per_dev = lanes // width
    modes_rows = forward.shape[1]
    kind = lambda k: (jnp.minimum(k, 1), 0, 0)
    whole3 = lambda k: (0, 0, 0)
    return pl.pallas_call(
        modes_kernel,
        grid=(per_dev,),
        out_shape=jax.ShapeDtypeStruct((rows, lanes), jnp.bfloat16),
        in_specs=[
            pl.BlockSpec((rows, width), lambda k: (0, k)),
            pl.BlockSpec((1,) + forward.shape[1:], kind),
            pl.BlockSpec(first.shape, whole3),
            pl.BlockSpec(second.shape, whole3),
            pl.BlockSpec(bias.shape, lambda k: (0, 0)),
            pl.BlockSpec((1,) + inverse.shape[1:], kind),
        ],
        out_specs=pl.BlockSpec((rows, width), lambda k: (0, k)),
        scratch_shapes=[pltpu.VMEM((modes_rows, width), jnp.bfloat16)],
        compiler_params=pltpu.CompilerParams(vmem_limit_bytes=60 * MIB),
        cost_estimate=pl.CostEstimate(
            flops=2 * lanes * (2 * rows * modes_rows + modes_rows * 512),
            bytes_accessed=4 * (rows * lanes + first.size),
            transcendentals=0,
        ),
        name="mix_modes",
    )(spectra, forward, first, second, bias, inverse)


def residual_kernel(spectra, table, tokens, gain, residual, *halves):
    width = tokens.shape[1]
    mixing = None
    for column in range(table.shape[0]):
        term = mxu(table[column], spectra[:, column * width : (column + 1) * width])
        mixing = term if mixing is None else mixing + term
    rounded = (tokens[...].astype(jnp.float32) + mixing).astype(jnp.bfloat16)
    residual[...] = rounded
    normed = normalize(rounded.astype(jnp.float32), gain[...]).astype(jnp.bfloat16)
    per_half = pl.num_programs(0) // len(halves)
    for index, half in enumerate(halves):

        @pl.when(pl.program_id(0) // per_half == index)
        def _(half=half):
            half[...] = normed


def half_tiles(tile, width, per_half, n_halves):
    return [
        pl.BlockSpec((tile, width), lambda i, first=index * per_half: (jnp.clip(i - first, 0, per_half - 1), 0))
        for index in range(n_halves)
    ]


def add_mixing(spectra, table, tokens, gain):
    per_dev, rows_out, rows_in = table.shape
    width = tokens.shape[1]
    tile = math.gcd(rows_out // 2, 256)
    steps = rows_out // tile
    row_tile = pl.BlockSpec((tile, width), lambda i: (i, 0))
    return pl.pallas_call(
        residual_kernel,
        grid=(steps,),
        out_shape=[jax.ShapeDtypeStruct((rows, width), jnp.bfloat16) for rows in (rows_out, rows_out // 2, rows_out // 2)],
        in_specs=[
            pl.BlockSpec(spectra.shape, lambda i: (0, 0)),
            pl.BlockSpec((per_dev, tile, rows_in), lambda i: (0, i, 0)),
            row_tile,
            pl.BlockSpec(gain.shape, lambda i: (0, 0)),
        ],
        out_specs=[row_tile] + half_tiles(tile, width, steps // 2, 2),
        compiler_params=pltpu.CompilerParams(vmem_limit_bytes=60 * MIB),
        cost_estimate=pl.CostEstimate(
            flops=2 * per_dev * rows_out * rows_in * width,
            bytes_accessed=2 * (3 * rows_out * width + spectra.size + table.size),
            transcendentals=0,
        ),
        name="add_mixing",
    )(spectra, table, tokens, gain)


def sum_kernel(residual, own, back_a, back_b, out):
    total = residual[...].astype(jnp.float32) + own[...]
    half = pl.num_programs(0) // 2
    for index, back in enumerate((back_a, back_b)):

        @pl.when(pl.program_id(0) // half == index)
        def _(back=back):
            out[...] = (total + back[...].astype(jnp.float32)).astype(out.dtype)


def add_outputs(residual, own, back_a, back_b):
    rows, width = residual.shape
    tile = math.gcd(rows // 2, 256)
    row_tile = pl.BlockSpec((tile, width), lambda i: (i, 0))
    return pl.pallas_call(
        sum_kernel,
        grid=(rows // tile,),
        out_shape=jax.ShapeDtypeStruct(residual.shape, jnp.bfloat16),
        in_specs=[row_tile, row_tile] + half_tiles(tile, width, rows // tile // 2, 2),
        out_specs=row_tile,
        compiler_params=pltpu.CompilerParams(vmem_limit_bytes=32 * MIB),
        name="add_outputs",
    )(residual, own, back_a, back_b)


def gate(value, *others):
    anywhere = pl.BlockSpec(memory_space=pl.ANY)
    return pl.pallas_call(
        lambda *refs: None,
        out_shape=jax.ShapeDtypeStruct(value.shape, value.dtype),
        in_specs=[anywhere] * (1 + len(others)),
        out_specs=anywhere,
        input_output_aliases={0: 0},
        compiler_params=pltpu.CompilerParams(vmem_limit_bytes=60 * MIB),
        cost_estimate=pl.CostEstimate(flops=10**11, bytes_accessed=10**8, transcendentals=0),
        name="gate",
    )(value, *others)


def gelu_twice(values):
    scale = math.sqrt(2.0 / math.pi)
    return values * jnp.tanh(values * (values * values * (0.044715 * scale) + scale)) + values


def experts_kernel(pieces, n_sets, n_outs, n_totals, chunk, weights, *refs):
    take = iter(refs)
    sets = [next(take) for _ in range(n_sets)]
    totals = [next(take) for _ in range(n_totals)]
    halves = [[next(take) for _ in range(count)] for count in pieces]
    outs = [next(take) for _ in range(n_outs)]
    values, up_all, down_all, set_sem, total_sem, piece_sem = (next(take) for _ in range(6))
    total = outs[0] if n_outs == 1 else next(take)
    n_blocks, _, hidden = up_all.shape
    tile = values.shape[0] // n_sets
    rows_of = lambda index: pl.ds(index * tile, tile)
    loads = [
        pltpu.make_async_copy(ref, values.at[rows_of(index)], set_sem.at[index]) for index, ref in enumerate(sets)
    ]
    total_loads = [
        pltpu.make_async_copy(ref, total.at[pl.ds(index * ref.shape[0], ref.shape[0])], total_sem.at[index])
        for index, ref in enumerate(totals)
    ]
    blocks = []
    piece = 0
    for block in range(n_blocks):
        copies = []
        for side in range(2):
            base = 0
            for ref in halves[2 * block + side]:
                size = ref.shape[1 - side]
                units = pl.ds(base, size)
                target = down_all.at[block, units, :] if side else up_all.at[block, :, units]
                copies.append(pltpu.make_async_copy(ref, target, piece_sem.at[piece]))
                base += size
                piece += 1
        blocks.append(copies)
    for copy in loads + blocks[0] + total_loads + blocks[1]:
        copy.start()
    for copy in loads:
        copy.wait()
    for block in range(n_blocks):
        for copy in blocks[block]:
            copy.wait()
        if 0 < block < n_blocks - 1:
            for copy in blocks[block + 1]:
                copy.start()
        if block == 0:
            for copy in total_loads:
                copy.wait()

        def token_tile(index, carry, block=block):
            rows = pl.ds(pl.multiple_of(index * tile, tile), tile)
            given = values[rows, :]
            acts = [
                gelu_twice(mxu(given, up_all[block, :, start : start + chunk])).astype(jnp.bfloat16)
                for start in range(0, hidden, chunk)
            ]
            term = mxu(jnp.concatenate(acts, axis=1), down_all[block]) * (0.5 * weights[rows, block : block + 1])
            if block > 0 or n_totals:
                term = total[rows, :] + term
            total[rows, :] = term
            return carry

        lax.fori_loop(0, n_sets, token_tile, 0)
    if n_outs > 1:
        for index, out in enumerate(outs):
            out[...] = total[index * tile : (index + 1) * tile, :].astype(out.dtype)


def run_experts(sets, weights, blocks, totals=(), split=False, chunk=256):
    rows, width = sets[0].shape
    halves = [half for block in blocks for half in block]
    weights_in = [piece for half in halves for piece in half]
    n_blocks = len(blocks)
    hidden = sum(piece.shape[1] for piece in blocks[0][0])
    chunk = math.gcd(chunk, hidden)
    n_rows = rows * len(sets)
    vmem = pl.BlockSpec(memory_space=pltpu.VMEM)
    anywhere = pl.BlockSpec(memory_space=pl.ANY)
    if split:
        out_shape = [jax.ShapeDtypeStruct((rows, width), jnp.bfloat16)] * len(sets)
    else:
        out_shape = [jax.ShapeDtypeStruct((n_rows, width), jnp.float32)]
    counts = tuple(len(half) for half in halves)
    return pl.pallas_call(
        functools.partial(experts_kernel, counts, len(sets), len(out_shape), len(totals), chunk),
        out_shape=out_shape,
        in_specs=[vmem] + [anywhere] * (len(sets) + len(totals) + len(weights_in)),
        out_specs=[vmem] * len(out_shape),
        scratch_shapes=[
            pltpu.VMEM((n_rows, width), jnp.bfloat16),
            pltpu.VMEM((n_blocks, width, hidden), jnp.bfloat16),
            pltpu.VMEM((n_blocks, hidden, width), jnp.bfloat16),
            pltpu.SemaphoreType.DMA((len(sets),)),
            pltpu.SemaphoreType.DMA((len(sets),)),
            pltpu.SemaphoreType.DMA((len(weights_in),)),
        ]
        + ([pltpu.VMEM((n_rows, width), jnp.float32)] if split else []),
        compiler_params=pltpu.CompilerParams(vmem_limit_bytes=60 * MIB),
        cost_estimate=pl.CostEstimate(
            flops=4 * n_rows * width * hidden * n_blocks,
            bytes_accessed=4 * width * hidden * n_blocks + 8 * n_rows * width,
            transcendentals=n_rows * hidden * n_blocks,
        ),
        name="experts",
    )(weights, *sets, *totals, *weights_in)


def expert_weights(routing, combine, n_experts):
    route, weight = (value.reshape(-1, value.shape[-1]) for value in (routing, combine))
    return jnp.stack([jnp.sum(jnp.where(route == e, weight, 0.0), axis=-1) for e in range(n_experts)])


def tie(value, *others):
    return lax.optimization_barrier((value, others))[0]


class Weights:
    def __init__(self, up, down):
        n_parts = lax.axis_size("group") * lax.axis_size("expert")
        part = lax.axis_index("group") * lax.axis_size("expert") + lax.axis_index("expert")
        size = up.shape[1] // n_parts
        self.own = ([up], [down])
        self.part = (
            lax.dynamic_slice_in_dim(up, part * size, size, axis=1),
            lax.dynamic_slice_in_dim(down, part * size, size, axis=0),
        )

    @staticmethod
    def spread(piece):
        other = exchange(piece, "group", 1)
        pieces = [piece, other, exchange(piece, "expert", 1), exchange(other, "expert", 1)]
        return tuple(list(side) for side in zip(*pieces))


def routed_experts(residual, normed, routing, combine, up_weight, down_weight):
    n_tokens, width = normed.shape
    top_count = routing.shape[-1]
    experts = lax.axis_size("row") // 2
    capacity = n_tokens * top_count // experts
    flat_route = routing.reshape(-1)
    one_hot = (flat_route[:, None] == jnp.arange(experts, dtype=jnp.int32)[None, :]).astype(jnp.int32)
    earlier = jnp.cumsum(one_hot, axis=0) - one_hot
    slot_index = flat_route * capacity + jnp.sum(earlier * one_hot, axis=1)
    token_of = jnp.arange(n_tokens * top_count, dtype=jnp.int32) // top_count
    source_row = jnp.zeros((experts * capacity,), jnp.int32).at[slot_index].set(token_of)
    send_rows = normed[source_row].reshape(experts, capacity, width)
    partner_up, partner_down = exchange((up_weight, down_weight), "row", 1)
    up_full = jnp.concatenate([up_weight[0], partner_up[0]], axis=1)
    down_full = jnp.concatenate([down_weight[0], partner_down[0]], axis=0)
    outgoing = send_rows.reshape(experts * 2, capacity // 2, width)
    arrived = lax.all_to_all(outgoing, "row", split_axis=0, concat_axis=0, tiled=True)
    hidden = jax.nn.gelu(mxu(arrived.reshape(-1, width), up_full), approximate=True).astype(jnp.bfloat16)
    partial_out = mxu(hidden, down_full).reshape(arrived.shape).astype(jnp.bfloat16)
    returned = lax.all_to_all(partial_out, "row", split_axis=0, concat_axis=0, tiled=True)
    gathered = returned.reshape(-1, width)[slot_index].reshape(n_tokens, top_count, width)
    scaled = gathered.astype(jnp.float32) * combine.reshape(n_tokens, top_count, 1)
    return residual.astype(jnp.float32) + jnp.sum(scaled, axis=1)


def complex_weight(weight):
    real, imag = weight[0], weight[1]
    return jnp.concatenate(
        [jnp.concatenate([real, imag], axis=2), jnp.concatenate([-imag, real], axis=2)], axis=1
    )


def per_device(
    tokens,
    ln_first,
    spec_first,
    spec_second,
    spec_bias,
    ln_second,
    routing,
    combine,
    up_weight,
    down_weight,
):
    _, rows_local, grid_len, width = tokens.shape
    axes = ("row", "expert")
    n_dev = lax.axis_size(axes)
    n_blocks = spec_first.shape[1]
    forward_cols, inverse_cols = column_tables(grid_len, n_dev, rows_local)
    forward_rows, inverse_rows = row_tables(grid_len)
    first_device = lax.axis_index(axes) == 0
    pick = lambda table: jnp.stack([jnp.where(first_device, table[0], table[1]), table[1]])
    flat_tokens = tokens.reshape(-1, width)

    spectra = column_spectra(flat_tokens, ln_first.reshape(1, width), jnp.asarray(forward_cols))
    by_column = lax.all_to_all(
        spectra.reshape(n_dev, -1, spectra.shape[1]), axes, split_axis=0, concat_axis=0, tiled=True
    )
    bias = spec_bias.reshape(2, n_blocks, -1).transpose(1, 0, 2).reshape(n_blocks, -1)
    gain = ln_second.reshape(1, width)
    pairs = lax.axis_size("group") == 2 and lax.axis_size("expert") == 2
    every_expert = lax.axis_size("row") == 2 * routing.shape[-1] and routing.shape[-1] == 4
    dense = pairs and every_expert
    if dense:
        weights = Weights(up_weight[0], down_weight[0])
        table = expert_weights(routing, combine, routing.shape[-1])
        half_size = table.shape[1] // 2
        arriving = [exchange(table[:, :half_size], "row", 1), exchange(table[:, half_size:], "row", 2)]
        near = exchange(weights.part, "row", 3)
        far_up = exchange(weights.part[0], "row", 4)
        bias = gate(bias, far_up, *near, *arriving)
    mixed = mix_modes(
        by_column.reshape(spectra.shape),
        pick(forward_rows),
        complex_weight(spec_first),
        complex_weight(spec_second),
        bias,
        pick(inverse_rows),
        width,
    )
    by_row = lax.all_to_all(
        mixed.reshape(n_dev, -1, mixed.shape[1]), axes, split_axis=0, concat_axis=0, tiled=True
    )
    if dense:
        near_all = Weights.spread(near)
        far_down = exchange(weights.part[1], "row", 4)
        far_near_up = exchange(far_up, "row", 3)
        gain = gate(gain, far_down, far_near_up, *near_all[0], *near_all[1])
    residual, norm_a, norm_b = add_mixing(
        by_row.reshape(mixed.shape), jnp.asarray(inverse_cols), flat_tokens, gain
    )
    if not dense:
        normed = jnp.concatenate([norm_a, norm_b])
        final = routed_experts(residual, normed, routing, combine, up_weight, down_weight)
        return final.astype(jnp.bfloat16).reshape(tokens.shape)

    from_y = exchange(norm_a, "row", 1)
    from_z = exchange(norm_b, "row", 2)
    far_near_down = exchange(far_down, "row", 3)
    far_all = Weights.spread((far_up, far_down))
    far_near_all = Weights.spread((far_near_up, far_near_down))
    expert = lax.axis_index("row") // 2
    pick_weights = lambda columns, numbers: jnp.stack(
        [lax.dynamic_index_in_dim(columns, expert ^ number, 0, keepdims=False) for number in numbers], axis=1
    )
    table_in = jnp.concatenate(arriving, axis=1)
    lower, upper = [weights.own, near_all], [far_all, far_near_all]
    (own,) = run_experts([norm_a, norm_b], pick_weights(table, (0, 1)), lower)
    back_y, back_z = run_experts([from_y, from_z], pick_weights(table_in, (0, 1, 2, 3)), lower + upper, split=True)
    back_a = exchange(back_y, "row", 1)
    back_b = exchange(back_z, "row", 2)
    (own,) = run_experts([norm_a, norm_b], pick_weights(table, (2, 3)), upper, [own])
    return add_outputs(residual, own, back_a, back_b).reshape(tokens.shape)


def solution(mesh):
    placed = (
        P("group", ("row", "expert"), None, None),
        P(),
        P(),
        P(),
        P(),
        P(),
        P("group", ("row", "expert"), None, None),
        P("group", ("row", "expert"), None, None),
        P("row", None, None),
        P("row", None, None),
    )
    return jax.shard_map(
        per_device,
        mesh=mesh,
        in_specs=placed,
        out_specs=P("group", ("row", "expert"), None, None),
        check_vma=False,
    )
```

```python
import functools
import math

import jax
import jax.numpy as jnp
import ml_dtypes
import numpy as np
from jax import lax
from jax.experimental import pallas as pl
from jax.experimental.pallas import tpu as pltpu
from jax.sharding import PartitionSpec as P

MIB = 1 << 20


def exchange(value, axis, mask):
    pairs = [(source, source ^ mask) for source in range(lax.axis_size(axis))]
    return lax.ppermute(value, axis, pairs)


def mxu(left, right):
    return jnp.dot(left, right, preferred_element_type=jnp.float32)


def normalize(values, gain):
    center = values - jnp.mean(values, axis=-1, keepdims=True)
    spread = jnp.mean(center * center, axis=-1, keepdims=True)
    return center * lax.rsqrt(spread + 1e-05) * gain


def trig(grid_len):
    counter = np.arange(grid_len)
    angle = 2.0 * math.pi / grid_len * (np.outer(counter, counter) % grid_len)
    cosine = np.round(np.cos(angle), 12).astype(ml_dtypes.bfloat16).astype(np.float64)
    sine = np.round(np.sin(angle), 12).astype(ml_dtypes.bfloat16).astype(np.float64)
    return cosine, sine


def column_tables(grid_len, n_dev, rows_local):
    cosine, sine = trig(grid_len)
    packed = grid_len // 2
    per_dev = packed // n_dev
    part = np.stack([cosine[:packed], -sine[:packed]], axis=1)
    part[0, 1] = cosine[packed]
    part = part.reshape(n_dev, per_dev, 2, grid_len)
    forward = np.zeros((per_dev, n_dev, rows_local, 2, rows_local, grid_len))
    for row in range(rows_local):
        forward[:, :, row, :, row, :] = part.transpose(1, 0, 2, 3)
    forward = forward.reshape(per_dev, n_dev * rows_local * 2, rows_local * grid_len)
    inverse = forward.transpose(0, 2, 1) / grid_len
    return forward.astype(ml_dtypes.bfloat16), inverse.astype(ml_dtypes.bfloat16)


def row_tables(grid_len):
    c, s = trig(grid_len)
    z = np.zeros_like(c)

    def assemble(blocks):
        array = np.array(blocks)
        return array.transpose(0, 1, 3, 4, 2).reshape(4 * grid_len, 2 * grid_len)

    plain_fwd = assemble([[[c, s], [-s, c]], [[c, -s], [-s, -c]]]) / grid_len
    first_fwd = assemble([[[c, z], [-s, z]], [[z, c], [z, -s]]]) / grid_len
    plain_inv = assemble([[[c, s], [-s, c]], [[c, -s], [-s, -c]]]).T
    first_inv = assemble([[[c, z], [-s, z]], [[z, c], [z, -s]]]).T
    kinds = lambda first, plain: np.stack([first, plain]).astype(ml_dtypes.bfloat16)
    return kinds(first_fwd, plain_fwd), kinds(first_inv, plain_inv)


def spectra_kernel(tokens, gain, table, out, normed):
    tile = 128
    width = tokens.shape[1]

    def norm_tile(index, carry):
        rows = pl.ds(pl.multiple_of(index * tile, tile), tile)
        values = tokens[rows, :].astype(jnp.float32)
        normed[rows, :] = normalize(values, gain[...]).astype(normed.dtype)
        return carry

    lax.fori_loop(0, tokens.shape[0] // tile, norm_tile, 0)
    for column in range(table.shape[0]):
        out[:, column * width : (column + 1) * width] = mxu(table[column], normed[...]).astype(out.dtype)


def column_spectra(tokens, gain, table):
    per_dev, rows_out, rows_in = table.shape
    width = tokens.shape[1]
    return pl.pallas_call(
        spectra_kernel,
        out_shape=jax.ShapeDtypeStruct((rows_out, per_dev * width), jnp.bfloat16),
        in_specs=[pl.BlockSpec(memory_space=pltpu.VMEM)] * 3,
        out_specs=pl.BlockSpec(memory_space=pltpu.VMEM),
        scratch_shapes=[pltpu.VMEM((rows_in, width), jnp.bfloat16)],
        compiler_params=pltpu.CompilerParams(vmem_limit_bytes=20 * MIB),
        cost_estimate=pl.CostEstimate(
            flops=2 * per_dev * rows_out * rows_in * width,
            bytes_accessed=2 * (rows_in * width + rows_out * per_dev * width + table.size),
            transcendentals=0,
        ),
        name="column_spectra",
    )(tokens, gain, table)


def modes_kernel(spectra, forward, first, second, bias, inverse, out, mixed):
    n_blocks, pair, _ = first.shape
    block = pair // 2
    grid_len = spectra.shape[0] // 2
    modes = mxu(forward[0], spectra[...]).astype(jnp.bfloat16)
    for index in range(n_blocks):
        lanes = slice(index * block, (index + 1) * block)
        sides = [
            jnp.concatenate(
                [
                    modes[2 * sign * grid_len : (2 * sign + 1) * grid_len, lanes],
                    modes[(2 * sign + 1) * grid_len : (2 * sign + 2) * grid_len, lanes],
                ],
                axis=1,
            )
            for sign in range(2)
        ]
        hid = mxu(jnp.concatenate(sides, axis=0), first[index])
        hid = jnp.maximum(hid + bias[index : index + 1, :], 0.0).astype(jnp.bfloat16)
        result = mxu(hid, second[index]).astype(jnp.bfloat16)
        for sign in range(2):
            for part in range(2):
                base = (2 * sign + part) * grid_len
                mixed[base : base + grid_len, lanes] = result[
                    sign * grid_len : (sign + 1) * grid_len, part * block : (part + 1) * block
                ]
    out[...] = mxu(inverse[0], mixed[...]).astype(out.dtype)


def mix_modes(spectra, forward, first, second, bias, inverse, width):
    rows, lanes = spectra.shape
    per_dev = lanes // width
    modes_rows = forward.shape[1]
    kind = lambda k: (jnp.minimum(k, 1), 0, 0)
    whole3 = lambda k: (0, 0, 0)
    return pl.pallas_call(
        modes_kernel,
        grid=(per_dev,),
        out_shape=jax.ShapeDtypeStruct((rows, lanes), jnp.bfloat16),
        in_specs=[
            pl.BlockSpec((rows, width), lambda k: (0, k)),
            pl.BlockSpec((1,) + forward.shape[1:], kind),
            pl.BlockSpec(first.shape, whole3),
            pl.BlockSpec(second.shape, whole3),
            pl.BlockSpec(bias.shape, lambda k: (0, 0)),
            pl.BlockSpec((1,) + inverse.shape[1:], kind),
        ],
        out_specs=pl.BlockSpec((rows, width), lambda k: (0, k)),
        scratch_shapes=[pltpu.VMEM((modes_rows, width), jnp.bfloat16)],
        compiler_params=pltpu.CompilerParams(vmem_limit_bytes=20 * MIB),
        cost_estimate=pl.CostEstimate(
            flops=2 * lanes * (2 * rows * modes_rows + modes_rows * 512),
            bytes_accessed=4 * (rows * lanes + first.size),
            transcendentals=0,
        ),
        name="mix_modes",
    )(spectra, forward, first, second, bias, inverse)


def residual_kernel(spectra, table, tokens, gain, residual, *halves):
    width = tokens.shape[1]
    mixing = None
    for column in range(table.shape[0]):
        term = mxu(table[column], spectra[:, column * width : (column + 1) * width])
        mixing = term if mixing is None else mixing + term
    rounded = (tokens[...].astype(jnp.float32) + mixing).astype(jnp.bfloat16)
    residual[...] = rounded
    normed = normalize(rounded.astype(jnp.float32), gain[...]).astype(jnp.bfloat16)
    per_half = pl.num_programs(0) // len(halves)
    for index, half in enumerate(halves):

        @pl.when(pl.program_id(0) // per_half == index)
        def _(half=half):
            half[...] = normed


def part_tiles(tile, width, per_part, n_parts):
    return [
        pl.BlockSpec((tile, width), lambda i, first=index * per_part: (jnp.clip(i - first, 0, per_part - 1), 0))
        for index in range(n_parts)
    ]


def add_mixing(spectra, table, tokens, gain, n_parts=4):
    per_dev, rows_out, rows_in = table.shape
    width = tokens.shape[1]
    tile = math.gcd(rows_out // n_parts, 256)
    steps = rows_out // tile
    row_tile = pl.BlockSpec((tile, width), lambda i: (i, 0))
    return pl.pallas_call(
        residual_kernel,
        grid=(steps,),
        out_shape=[jax.ShapeDtypeStruct((rows, width), jnp.bfloat16) for rows in [rows_out] + n_parts * [rows_out // n_parts]],
        in_specs=[
            pl.BlockSpec(spectra.shape, lambda i: (0, 0)),
            pl.BlockSpec((per_dev, tile, rows_in), lambda i: (0, i, 0)),
            row_tile,
            pl.BlockSpec(gain.shape, lambda i: (0, 0)),
        ],
        out_specs=[row_tile] + part_tiles(tile, width, steps // n_parts, n_parts),
        compiler_params=pltpu.CompilerParams(vmem_limit_bytes=20 * MIB),
        cost_estimate=pl.CostEstimate(
            flops=2 * per_dev * rows_out * rows_in * width,
            bytes_accessed=2 * (3 * rows_out * width + spectra.size + table.size),
            transcendentals=0,
        ),
        name="add_mixing",
    )(spectra, table, tokens, gain)


def sum_kernel(residual, own, *refs):
    backs, out = refs[:-1], refs[-1]
    total = residual[...].astype(jnp.float32) + own[...]
    per_part = pl.num_programs(0) // len(backs)
    for index, back in enumerate(backs):

        @pl.when(pl.program_id(0) // per_part == index)
        def _(back=back):
            out[...] = (total + back[...].astype(jnp.float32)).astype(out.dtype)


def add_outputs(residual, own, backs):
    rows, width = residual.shape
    tile = math.gcd(rows // len(backs), 256)
    row_tile = pl.BlockSpec((tile, width), lambda i: (i, 0))
    return pl.pallas_call(
        sum_kernel,
        grid=(rows // tile,),
        out_shape=jax.ShapeDtypeStruct(residual.shape, jnp.bfloat16),
        in_specs=[row_tile, row_tile] + part_tiles(tile, width, rows // tile // len(backs), len(backs)),
        out_specs=row_tile,
        compiler_params=pltpu.CompilerParams(vmem_limit_bytes=16 * MIB),
        name="add_outputs",
    )(residual, own, *backs)


def gate(value, *others):
    anywhere = pl.BlockSpec(memory_space=pl.ANY)
    return pl.pallas_call(
        lambda *refs: None,
        out_shape=jax.ShapeDtypeStruct(value.shape, value.dtype),
        in_specs=[anywhere] * (1 + len(others)),
        out_specs=anywhere,
        input_output_aliases={0: 0},
        compiler_params=pltpu.CompilerParams(vmem_limit_bytes=MIB),
        cost_estimate=pl.CostEstimate(flops=10**11, bytes_accessed=10**8, transcendentals=0),
        name="gate",
    )(value, *others)


def gelu_twice(values):
    scale = math.sqrt(2.0 / math.pi)
    return values * jnp.tanh(values * (values * values * (0.044715 * scale) + scale)) + values


def experts_kernel(pieces, n_sets, n_outs, n_totals, chunk, weights, *refs):
    take = iter(refs)
    sets = [next(take) for _ in range(n_sets)]
    totals = [next(take) for _ in range(n_totals)]
    halves = [[next(take) for _ in range(count)] for count in pieces]
    outs = [next(take) for _ in range(n_outs)]
    values, up_all, down_all, set_sem, total_sem, piece_sem = (next(take) for _ in range(6))
    total = outs[0] if n_outs == 1 else next(take)
    n_blocks, _, hidden = up_all.shape
    tile = math.gcd(values.shape[0], 512)
    set_size = values.shape[0] // n_sets
    rows_of = lambda index: pl.ds(index * set_size, set_size)
    loads = [
        pltpu.make_async_copy(ref, values.at[rows_of(index)], set_sem.at[index]) for index, ref in enumerate(sets)
    ]
    total_loads = [
        pltpu.make_async_copy(ref, total.at[pl.ds(index * ref.shape[0], ref.shape[0])], total_sem.at[index])
        for index, ref in enumerate(totals)
    ]
    blocks = []
    piece = 0
    for block in range(n_blocks):
        copies = []
        for side in range(2):
            base = 0
            for ref in halves[2 * block + side]:
                size = ref.shape[1 - side]
                units = pl.ds(base, size)
                target = down_all.at[block, units, :] if side else up_all.at[block, :, units]
                copies.append(pltpu.make_async_copy(ref, target, piece_sem.at[piece]))
                base += size
                piece += 1
        blocks.append(copies)
    for copy in loads + blocks[0] + total_loads + blocks[1]:
        copy.start()
    for copy in loads:
        copy.wait()
    for block in range(n_blocks):
        for copy in blocks[block]:
            copy.wait()
        if 0 < block < n_blocks - 1:
            for copy in blocks[block + 1]:
                copy.start()
        if block == 0:
            for copy in total_loads:
                copy.wait()

        def token_tile(index, carry, block=block):
            rows = pl.ds(pl.multiple_of(index * tile, tile), tile)
            given = values[rows, :]
            acts = [
                gelu_twice(mxu(given, up_all[block, :, start : start + chunk])).astype(jnp.bfloat16)
                for start in range(0, hidden, chunk)
            ]
            term = mxu(jnp.concatenate(acts, axis=1), down_all[block]) * (0.5 * weights[rows, block : block + 1])
            if block > 0 or n_totals:
                term = total[rows, :] + term
            total[rows, :] = term
            return carry

        lax.fori_loop(0, values.shape[0] // tile, token_tile, 0)
    if n_outs > 1:
        for index, out in enumerate(outs):
            out[...] = total[index * set_size : (index + 1) * set_size, :].astype(out.dtype)


def run_experts(sets, weights, blocks, totals=(), split=False, chunk=256):
    rows, width = sets[0].shape
    halves = [half for block in blocks for half in block]
    weights_in = [piece for half in halves for piece in half]
    n_blocks = len(blocks)
    hidden = sum(piece.shape[1] for piece in blocks[0][0])
    chunk = math.gcd(chunk, hidden)
    n_rows = rows * len(sets)
    vmem = pl.BlockSpec(memory_space=pltpu.VMEM)
    anywhere = pl.BlockSpec(memory_space=pl.ANY)
    if split:
        out_shape = [jax.ShapeDtypeStruct((rows, width), jnp.bfloat16)] * len(sets)
    else:
        out_shape = [jax.ShapeDtypeStruct((n_rows, width), jnp.float32)]
    counts = tuple(len(half) for half in halves)
    used = n_blocks * 4 * width * hidden + 2 * n_rows * width + 4 * n_rows * width + (2 * n_rows * width if split else 0)
    return pl.pallas_call(
        functools.partial(experts_kernel, counts, len(sets), len(out_shape), len(totals), chunk),
        out_shape=out_shape,
        in_specs=[vmem] + [anywhere] * (len(sets) + len(totals) + len(weights_in)),
        out_specs=[vmem] * len(out_shape),
        scratch_shapes=[
            pltpu.VMEM((n_rows, width), jnp.bfloat16),
            pltpu.VMEM((n_blocks, width, hidden), jnp.bfloat16),
            pltpu.VMEM((n_blocks, hidden, width), jnp.bfloat16),
            pltpu.SemaphoreType.DMA((len(sets),)),
            pltpu.SemaphoreType.DMA((len(sets),)),
            pltpu.SemaphoreType.DMA((len(weights_in),)),
        ]
        + ([pltpu.VMEM((n_rows, width), jnp.float32)] if split else []),
        compiler_params=pltpu.CompilerParams(vmem_limit_bytes=used + 4 * MIB),
        cost_estimate=pl.CostEstimate(
            flops=4 * n_rows * width * hidden * n_blocks,
            bytes_accessed=4 * width * hidden * n_blocks + 8 * n_rows * width,
            transcendentals=n_rows * hidden * n_blocks,
        ),
        name="experts",
    )(weights, *sets, *totals, *weights_in)


def expert_weights(routing, combine, n_experts):
    route, weight = (value.reshape(-1, value.shape[-1]) for value in (routing, combine))
    return jnp.stack([jnp.sum(jnp.where(route == e, weight, 0.0), axis=-1) for e in range(n_experts)])


def tie(value, *others):
    return lax.optimization_barrier((value, others))[0]


class Weights:
    def __init__(self, up, down):
        n_parts = lax.axis_size("group") * lax.axis_size("expert")
        part = lax.axis_index("group") * lax.axis_size("expert") + lax.axis_index("expert")
        size = up.shape[1] // n_parts
        self.own = ([up], [down])
        self.part = (
            lax.dynamic_slice_in_dim(up, part * size, size, axis=1),
            lax.dynamic_slice_in_dim(down, part * size, size, axis=0),
        )

    @staticmethod
    def spread(piece):
        other = exchange(piece, "group", 1)
        pieces = [piece, other, exchange(piece, "expert", 1), exchange(other, "expert", 1)]
        return tuple(list(side) for side in zip(*pieces))


def routed_experts(residual, normed, routing, combine, up_weight, down_weight):
    n_tokens, width = normed.shape
    top_count = routing.shape[-1]
    experts = lax.axis_size("row") // 2
    capacity = n_tokens * top_count // experts
    flat_route = routing.reshape(-1)
    one_hot = (flat_route[:, None] == jnp.arange(experts, dtype=jnp.int32)[None, :]).astype(jnp.int32)
    earlier = jnp.cumsum(one_hot, axis=0) - one_hot
    slot_index = flat_route * capacity + jnp.sum(earlier * one_hot, axis=1)
    token_of = jnp.arange(n_tokens * top_count, dtype=jnp.int32) // top_count
    source_row = jnp.zeros((experts * capacity,), jnp.int32).at[slot_index].set(token_of)
    send_rows = normed[source_row].reshape(experts, capacity, width)
    partner_up, partner_down = exchange((up_weight, down_weight), "row", 1)
    up_full = jnp.concatenate([up_weight[0], partner_up[0]], axis=1)
    down_full = jnp.concatenate([down_weight[0], partner_down[0]], axis=0)
    outgoing = send_rows.reshape(experts * 2, capacity // 2, width)
    arrived = lax.all_to_all(outgoing, "row", split_axis=0, concat_axis=0, tiled=True)
    hidden = jax.nn.gelu(mxu(arrived.reshape(-1, width), up_full), approximate=True).astype(jnp.bfloat16)
    partial_out = mxu(hidden, down_full).reshape(arrived.shape).astype(jnp.bfloat16)
    returned = lax.all_to_all(partial_out, "row", split_axis=0, concat_axis=0, tiled=True)
    gathered = returned.reshape(-1, width)[slot_index].reshape(n_tokens, top_count, width)
    scaled = gathered.astype(jnp.float32) * combine.reshape(n_tokens, top_count, 1)
    return residual.astype(jnp.float32) + jnp.sum(scaled, axis=1)


def complex_weight(weight):
    real, imag = weight[0], weight[1]
    return jnp.concatenate(
        [jnp.concatenate([real, imag], axis=2), jnp.concatenate([-imag, real], axis=2)], axis=1
    )


def per_device(
    tokens,
    ln_first,
    spec_first,
    spec_second,
    spec_bias,
    ln_second,
    routing,
    combine,
    up_weight,
    down_weight,
):
    _, rows_local, grid_len, width = tokens.shape
    axes = ("row", "expert")
    n_dev = lax.axis_size(axes)
    n_blocks = spec_first.shape[1]
    forward_cols, inverse_cols = column_tables(grid_len, n_dev, rows_local)
    forward_rows, inverse_rows = row_tables(grid_len)
    first_device = lax.axis_index(axes) == 0
    pick = lambda table: jnp.stack([jnp.where(first_device, table[0], table[1]), table[1]])
    flat_tokens = tokens.reshape(-1, width)

    spectra = column_spectra(flat_tokens, ln_first.reshape(1, width), jnp.asarray(forward_cols))
    by_column = lax.all_to_all(
        spectra.reshape(n_dev, -1, spectra.shape[1]), axes, split_axis=0, concat_axis=0, tiled=True
    )
    bias = spec_bias.reshape(2, n_blocks, -1).transpose(1, 0, 2).reshape(n_blocks, -1)
    gain = ln_second.reshape(1, width)
    pairs = lax.axis_size("group") == 2 and lax.axis_size("expert") == 2
    every_expert = lax.axis_size("row") == 2 * routing.shape[-1] and routing.shape[-1] == 4
    dense = pairs and every_expert
    if dense:
        weights = Weights(up_weight[0], down_weight[0])
        table = expert_weights(routing, combine, routing.shape[-1])
        half_size = table.shape[1] // 2
        arriving = [exchange(table[:, :half_size], "row", 1), exchange(table[:, half_size:], "row", 2)]
        near = exchange(weights.part, "row", 3)
        far_up = exchange(weights.part[0], "row", 4)
        bias = gate(bias, far_up, *near)
    mixed = mix_modes(
        by_column.reshape(spectra.shape),
        pick(forward_rows),
        complex_weight(spec_first),
        complex_weight(spec_second),
        bias,
        pick(inverse_rows),
        width,
    )
    by_row = lax.all_to_all(
        mixed.reshape(n_dev, -1, mixed.shape[1]), axes, split_axis=0, concat_axis=0, tiled=True
    )
    if dense:
        near_all = Weights.spread(near)
        far_down = exchange(weights.part[1], "row", 4)
        far_near_up = exchange(far_up, "row", 3)
        gain = gate(gain, far_down, far_near_up, *near_all[0], *near_all[1], *arriving)
    residual, *norms = add_mixing(
        by_row.reshape(mixed.shape), jnp.asarray(inverse_cols), flat_tokens, gain
    )
    if not dense:
        normed = jnp.concatenate(norms)
        final = routed_experts(residual, normed, routing, combine, up_weight, down_weight)
        return final.astype(jnp.bfloat16).reshape(tokens.shape)

    per_row = len(norms) // 2
    rows_of = [1] * per_row + [2] * per_row
    others = [exchange(norm, "row", mask) for norm, mask in zip(norms, rows_of)]
    far_near_down = exchange(far_down, "row", 3)
    far_all = Weights.spread((far_up, far_down))
    far_near_all = Weights.spread((far_near_up, far_near_down))
    expert = lax.axis_index("row") // 2
    pick_weights = lambda columns, numbers: jnp.stack(
        [lax.dynamic_index_in_dim(columns, expert ^ number, 0, keepdims=False) for number in numbers], axis=1
    )
    lower, upper = [weights.own, near_all], [far_all, far_near_all]
    (own,) = run_experts(norms, pick_weights(table, (0, 1)), lower)
    backs = [None] * len(norms)
    size = norms[0].shape[0]
    for index in range(per_row):
        sets = (index, index + per_row)
        table_in = jnp.concatenate([side[:, index * size : (index + 1) * size] for side in arriving], axis=1)
        results = run_experts([others[k] for k in sets], pick_weights(table_in, (0, 1, 2, 3)), lower + upper, split=True)
        for k, result in zip(sets, results):
            backs[k] = exchange(result, "row", rows_of[k])
    (own,) = run_experts(norms, pick_weights(table, (2, 3)), upper, [own])
    return add_outputs(residual, own, backs).reshape(tokens.shape)


def solution(mesh):
    placed = (
        P("group", ("row", "expert"), None, None),
        P(),
        P(),
        P(),
        P(),
        P(),
        P("group", ("row", "expert"), None, None),
        P("group", ("row", "expert"), None, None),
        P("row", None, None),
        P("row", None, None),
    )
    return jax.shard_map(
        per_device,
        mesh=mesh,
        in_specs=placed,
        out_specs=P("group", ("row", "expert"), None, None),
        check_vma=False,
    )
```

```python
import functools
import math

import jax
import jax.numpy as jnp
import ml_dtypes
import numpy as np
from jax import lax
from jax.experimental import pallas as pl
from jax.experimental.pallas import tpu as pltpu
from jax.sharding import PartitionSpec as P

MIB = 1 << 20


def exchange(value, axis, mask):
    pairs = [(source, source ^ mask) for source in range(lax.axis_size(axis))]
    return lax.ppermute(value, axis, pairs)


def mxu(left, right):
    return jnp.dot(left, right, preferred_element_type=jnp.float32)


def normalize(values, gain):
    center = values - jnp.mean(values, axis=-1, keepdims=True)
    spread = jnp.mean(center * center, axis=-1, keepdims=True)
    return center * lax.rsqrt(spread + 1e-05) * gain


def trig(grid_len):
    counter = np.arange(grid_len)
    angle = 2.0 * math.pi / grid_len * (np.outer(counter, counter) % grid_len)
    cosine = np.round(np.cos(angle), 12).astype(ml_dtypes.bfloat16).astype(np.float64)
    sine = np.round(np.sin(angle), 12).astype(ml_dtypes.bfloat16).astype(np.float64)
    return cosine, sine


def column_tables(grid_len, n_dev, rows_local):
    cosine, sine = trig(grid_len)
    packed = grid_len // 2
    per_dev = packed // n_dev
    part = np.stack([cosine[:packed], -sine[:packed]], axis=1)
    part[0, 1] = cosine[packed]
    part = part.reshape(n_dev, per_dev, 2, grid_len)
    forward = np.zeros((per_dev, n_dev, rows_local, 2, rows_local, grid_len))
    for row in range(rows_local):
        forward[:, :, row, :, row, :] = part.transpose(1, 0, 2, 3)
    forward = forward.reshape(per_dev, n_dev * rows_local * 2, rows_local * grid_len)
    inverse = forward.transpose(0, 2, 1) / grid_len
    return forward.astype(ml_dtypes.bfloat16), inverse.astype(ml_dtypes.bfloat16)


def row_tables(grid_len):
    c, s = trig(grid_len)
    z = np.zeros_like(c)

    def assemble(blocks):
        array = np.array(blocks)
        return array.transpose(0, 1, 3, 4, 2).reshape(4 * grid_len, 2 * grid_len)

    plain_fwd = assemble([[[c, s], [-s, c]], [[c, -s], [-s, -c]]]) / grid_len
    first_fwd = assemble([[[c, z], [-s, z]], [[z, c], [z, -s]]]) / grid_len
    plain_inv = assemble([[[c, s], [-s, c]], [[c, -s], [-s, -c]]]).T
    first_inv = assemble([[[c, z], [-s, z]], [[z, c], [z, -s]]]).T
    kinds = lambda first, plain: np.stack([first, plain]).astype(ml_dtypes.bfloat16)
    return kinds(first_fwd, plain_fwd), kinds(first_inv, plain_inv)


def spectra_kernel(tokens, gain, table, out, normed):
    tile = 128
    width = tokens.shape[1]

    def norm_tile(index, carry):
        rows = pl.ds(pl.multiple_of(index * tile, tile), tile)
        values = tokens[rows, :].astype(jnp.float32)
        normed[rows, :] = normalize(values, gain[...]).astype(normed.dtype)
        return carry

    lax.fori_loop(0, tokens.shape[0] // tile, norm_tile, 0)
    for column in range(table.shape[0]):
        out[:, column * width : (column + 1) * width] = mxu(table[column], normed[...]).astype(out.dtype)


def column_spectra(tokens, gain, table):
    per_dev, rows_out, rows_in = table.shape
    width = tokens.shape[1]
    return pl.pallas_call(
        spectra_kernel,
        out_shape=jax.ShapeDtypeStruct((rows_out, per_dev * width), jnp.bfloat16),
        in_specs=[pl.BlockSpec(memory_space=pltpu.VMEM)] * 3,
        out_specs=pl.BlockSpec(memory_space=pltpu.VMEM),
        scratch_shapes=[pltpu.VMEM((rows_in, width), jnp.bfloat16)],
        compiler_params=pltpu.CompilerParams(vmem_limit_bytes=20 * MIB),
        cost_estimate=pl.CostEstimate(
            flops=2 * per_dev * rows_out * rows_in * width,
            bytes_accessed=2 * (rows_in * width + rows_out * per_dev * width + table.size),
            transcendentals=0,
        ),
        name="column_spectra",
    )(tokens, gain, table)


def modes_kernel(spectra, forward, first, second, bias, inverse, out, mixed):
    n_blocks, pair, _ = first.shape
    block = pair // 2
    grid_len = spectra.shape[0] // 2
    modes = mxu(forward[0], spectra[...]).astype(jnp.bfloat16)
    for index in range(n_blocks):
        lanes = slice(index * block, (index + 1) * block)
        sides = [
            jnp.concatenate(
                [
                    modes[2 * sign * grid_len : (2 * sign + 1) * grid_len, lanes],
                    modes[(2 * sign + 1) * grid_len : (2 * sign + 2) * grid_len, lanes],
                ],
                axis=1,
            )
            for sign in range(2)
        ]
        hid = mxu(jnp.concatenate(sides, axis=0), first[index])
        hid = jnp.maximum(hid + bias[index : index + 1, :], 0.0).astype(jnp.bfloat16)
        result = mxu(hid, second[index]).astype(jnp.bfloat16)
        for sign in range(2):
            for part in range(2):
                base = (2 * sign + part) * grid_len
                mixed[base : base + grid_len, lanes] = result[
                    sign * grid_len : (sign + 1) * grid_len, part * block : (part + 1) * block
                ]
    out[...] = mxu(inverse[0], mixed[...]).astype(out.dtype)


def mix_modes(spectra, forward, first, second, bias, inverse, width):
    rows, lanes = spectra.shape
    per_dev = lanes // width
    modes_rows = forward.shape[1]
    kind = lambda k: (jnp.minimum(k, 1), 0, 0)
    whole3 = lambda k: (0, 0, 0)
    return pl.pallas_call(
        modes_kernel,
        grid=(per_dev,),
        out_shape=jax.ShapeDtypeStruct((rows, lanes), jnp.bfloat16),
        in_specs=[
            pl.BlockSpec((rows, width), lambda k: (0, k)),
            pl.BlockSpec((1,) + forward.shape[1:], kind),
            pl.BlockSpec(first.shape, whole3),
            pl.BlockSpec(second.shape, whole3),
            pl.BlockSpec(bias.shape, lambda k: (0, 0)),
            pl.BlockSpec((1,) + inverse.shape[1:], kind),
        ],
        out_specs=pl.BlockSpec((rows, width), lambda k: (0, k)),
        scratch_shapes=[pltpu.VMEM((modes_rows, width), jnp.bfloat16)],
        compiler_params=pltpu.CompilerParams(vmem_limit_bytes=20 * MIB),
        cost_estimate=pl.CostEstimate(
            flops=2 * lanes * (2 * rows * modes_rows + modes_rows * 512),
            bytes_accessed=4 * (rows * lanes + first.size),
            transcendentals=0,
        ),
        name="mix_modes",
    )(spectra, forward, first, second, bias, inverse)


def residual_kernel(spectra, table, tokens, gain, residual, *halves):
    width = tokens.shape[1]
    mixing = None
    for column in range(table.shape[0]):
        term = mxu(table[column], spectra[:, column * width : (column + 1) * width])
        mixing = term if mixing is None else mixing + term
    rounded = (tokens[...].astype(jnp.float32) + mixing).astype(jnp.bfloat16)
    residual[...] = rounded
    normed = normalize(rounded.astype(jnp.float32), gain[...]).astype(jnp.bfloat16)
    per_half = pl.num_programs(0) // len(halves)
    for index, half in enumerate(halves):

        @pl.when(pl.program_id(0) // per_half == index)
        def _(half=half):
            half[...] = normed


def part_tiles(tile, width, per_part, n_parts):
    return [
        pl.BlockSpec((tile, width), lambda i, first=index * per_part: (jnp.clip(i - first, 0, per_part - 1), 0))
        for index in range(n_parts)
    ]


def add_mixing(spectra, table, tokens, gain, n_parts=4):
    per_dev, rows_out, rows_in = table.shape
    width = tokens.shape[1]
    tile = math.gcd(rows_out // n_parts, 256)
    steps = rows_out // tile
    row_tile = pl.BlockSpec((tile, width), lambda i: (i, 0))
    return pl.pallas_call(
        residual_kernel,
        grid=(steps,),
        out_shape=[jax.ShapeDtypeStruct((rows, width), jnp.bfloat16) for rows in [rows_out] + n_parts * [rows_out // n_parts]],
        in_specs=[
            pl.BlockSpec(spectra.shape, lambda i: (0, 0)),
            pl.BlockSpec((per_dev, tile, rows_in), lambda i: (0, i, 0)),
            row_tile,
            pl.BlockSpec(gain.shape, lambda i: (0, 0)),
        ],
        out_specs=[row_tile] + part_tiles(tile, width, steps // n_parts, n_parts),
        compiler_params=pltpu.CompilerParams(vmem_limit_bytes=20 * MIB),
        cost_estimate=pl.CostEstimate(
            flops=2 * per_dev * rows_out * rows_in * width,
            bytes_accessed=2 * (3 * rows_out * width + spectra.size + table.size),
            transcendentals=0,
        ),
        name="add_mixing",
    )(spectra, table, tokens, gain)


def sum_kernel(residual, own, *refs):
    backs, out = refs[:-1], refs[-1]
    total = residual[...].astype(jnp.float32) + own[...]
    per_part = pl.num_programs(0) // len(backs)
    for index, back in enumerate(backs):

        @pl.when(pl.program_id(0) // per_part == index)
        def _(back=back):
            out[...] = (total + back[...].astype(jnp.float32)).astype(out.dtype)


def add_outputs(residual, own, backs):
    rows, width = residual.shape
    tile = math.gcd(rows // len(backs), 256)
    row_tile = pl.BlockSpec((tile, width), lambda i: (i, 0))
    return pl.pallas_call(
        sum_kernel,
        grid=(rows // tile,),
        out_shape=jax.ShapeDtypeStruct(residual.shape, jnp.bfloat16),
        in_specs=[row_tile, row_tile] + part_tiles(tile, width, rows // tile // len(backs), len(backs)),
        out_specs=row_tile,
        compiler_params=pltpu.CompilerParams(vmem_limit_bytes=16 * MIB),
        name="add_outputs",
    )(residual, own, *backs)


def gate(value, *others):
    anywhere = pl.BlockSpec(memory_space=pl.ANY)
    return pl.pallas_call(
        lambda *refs: None,
        out_shape=jax.ShapeDtypeStruct(value.shape, value.dtype),
        in_specs=[anywhere] * (1 + len(others)),
        out_specs=anywhere,
        input_output_aliases={0: 0},
        compiler_params=pltpu.CompilerParams(vmem_limit_bytes=MIB),
        cost_estimate=pl.CostEstimate(flops=10**11, bytes_accessed=10**8, transcendentals=0),
        name="gate",
    )(value, *others)


def gelu_twice(values):
    scale = math.sqrt(2.0 / math.pi)
    return values * jnp.tanh(values * (values * values * (0.044715 * scale) + scale)) + values


def experts_kernel(pieces, n_sets, n_outs, n_totals, chunk, weights, *refs):
    take = iter(refs)
    sets = [next(take) for _ in range(n_sets)]
    totals = [next(take) for _ in range(n_totals)]
    halves = [[next(take) for _ in range(count)] for count in pieces]
    outs = [next(take) for _ in range(n_outs)]
    values, up_all, down_all, set_sem, total_sem, piece_sem = (next(take) for _ in range(6))
    total = outs[0] if n_outs == 1 else next(take)
    n_blocks, _, hidden = up_all.shape
    tile = math.gcd(values.shape[0], 512)
    set_size = values.shape[0] // n_sets
    rows_of = lambda index: pl.ds(index * set_size, set_size)
    loads = [
        pltpu.make_async_copy(ref, values.at[rows_of(index)], set_sem.at[index]) for index, ref in enumerate(sets)
    ]
    total_loads = [
        pltpu.make_async_copy(ref, total.at[pl.ds(index * ref.shape[0], ref.shape[0])], total_sem.at[index])
        for index, ref in enumerate(totals)
    ]
    blocks = []
    piece = 0
    for block in range(n_blocks):
        copies = []
        for side in range(2):
            base = 0
            for ref in halves[2 * block + side]:
                size = ref.shape[1 - side]
                units = pl.ds(base, size)
                target = down_all.at[block, units, :] if side else up_all.at[block, :, units]
                copies.append(pltpu.make_async_copy(ref, target, piece_sem.at[piece]))
                base += size
                piece += 1
        blocks.append(copies)
    for copy in loads + blocks[0] + total_loads + blocks[1]:
        copy.start()
    for copy in loads:
        copy.wait()
    for block in range(n_blocks):
        for copy in blocks[block]:
            copy.wait()
        if 0 < block < n_blocks - 1:
            for copy in blocks[block + 1]:
                copy.start()
        if block == 0:
            for copy in total_loads:
                copy.wait()

        def token_tile(index, carry, block=block):
            rows = pl.ds(pl.multiple_of(index * tile, tile), tile)
            given = values[rows, :]
            acts = [
                gelu_twice(mxu(given, up_all[block, :, start : start + chunk])).astype(jnp.bfloat16)
                for start in range(0, hidden, chunk)
            ]
            term = mxu(jnp.concatenate(acts, axis=1), down_all[block]) * (0.5 * weights[rows, block : block + 1])
            if block > 0 or n_totals:
                term = total[rows, :] + term
            total[rows, :] = term
            return carry

        lax.fori_loop(0, values.shape[0] // tile, token_tile, 0)
    if n_outs > 1:
        for index, out in enumerate(outs):
            out[...] = total[index * set_size : (index + 1) * set_size, :].astype(out.dtype)


def run_experts(sets, weights, blocks, totals=(), split=False, chunk=256):
    rows, width = sets[0].shape
    halves = [half for block in blocks for half in block]
    weights_in = [piece for half in halves for piece in half]
    n_blocks = len(blocks)
    hidden = sum(piece.shape[1] for piece in blocks[0][0])
    chunk = math.gcd(chunk, hidden)
    n_rows = rows * len(sets)
    vmem = pl.BlockSpec(memory_space=pltpu.VMEM)
    anywhere = pl.BlockSpec(memory_space=pl.ANY)
    if split:
        out_shape = [jax.ShapeDtypeStruct((rows, width), jnp.bfloat16)] * len(sets)
    else:
        out_shape = [jax.ShapeDtypeStruct((n_rows, width), jnp.float32)]
    counts = tuple(len(half) for half in halves)
    used = n_blocks * 4 * width * hidden + 2 * n_rows * width + 4 * n_rows * width + (2 * n_rows * width if split else 0)
    return pl.pallas_call(
        functools.partial(experts_kernel, counts, len(sets), len(out_shape), len(totals), chunk),
        out_shape=out_shape,
        in_specs=[vmem] + [anywhere] * (len(sets) + len(totals) + len(weights_in)),
        out_specs=[vmem] * len(out_shape),
        scratch_shapes=[
            pltpu.VMEM((n_rows, width), jnp.bfloat16),
            pltpu.VMEM((n_blocks, width, hidden), jnp.bfloat16),
            pltpu.VMEM((n_blocks, hidden, width), jnp.bfloat16),
            pltpu.SemaphoreType.DMA((len(sets),)),
            pltpu.SemaphoreType.DMA((len(sets),)),
            pltpu.SemaphoreType.DMA((len(weights_in),)),
        ]
        + ([pltpu.VMEM((n_rows, width), jnp.float32)] if split else []),
        compiler_params=pltpu.CompilerParams(vmem_limit_bytes=used + 4 * MIB),
        cost_estimate=pl.CostEstimate(
            flops=4 * n_rows * width * hidden * n_blocks,
            bytes_accessed=4 * width * hidden * n_blocks + 8 * n_rows * width,
            transcendentals=n_rows * hidden * n_blocks,
        ),
        name="experts",
    )(weights, *sets, *totals, *weights_in)


def expert_weights(routing, combine, n_experts):
    route, weight = (value.reshape(-1, value.shape[-1]) for value in (routing, combine))
    return jnp.stack([jnp.sum(jnp.where(route == e, weight, 0.0), axis=-1) for e in range(n_experts)])


def tie(value, *others):
    return lax.optimization_barrier((value, others))[0]


class Weights:
    def __init__(self, up, down):
        n_parts = lax.axis_size("group") * lax.axis_size("expert")
        part = lax.axis_index("group") * lax.axis_size("expert") + lax.axis_index("expert")
        size = up.shape[1] // n_parts
        self.own = ([up], [down])
        self.part = (
            lax.dynamic_slice_in_dim(up, part * size, size, axis=1),
            lax.dynamic_slice_in_dim(down, part * size, size, axis=0),
        )

    @staticmethod
    def spread(piece):
        other = exchange(piece, "group", 1)
        pieces = [piece, other, exchange(piece, "expert", 1), exchange(other, "expert", 1)]
        return tuple(list(side) for side in zip(*pieces))


def routed_experts(residual, normed, routing, combine, up_weight, down_weight):
    n_tokens, width = normed.shape
    top_count = routing.shape[-1]
    experts = lax.axis_size("row") // 2
    capacity = n_tokens * top_count // experts
    flat_route = routing.reshape(-1)
    one_hot = (flat_route[:, None] == jnp.arange(experts, dtype=jnp.int32)[None, :]).astype(jnp.int32)
    earlier = jnp.cumsum(one_hot, axis=0) - one_hot
    slot_index = flat_route * capacity + jnp.sum(earlier * one_hot, axis=1)
    token_of = jnp.arange(n_tokens * top_count, dtype=jnp.int32) // top_count
    source_row = jnp.zeros((experts * capacity,), jnp.int32).at[slot_index].set(token_of)
    send_rows = normed[source_row].reshape(experts, capacity, width)
    partner_up, partner_down = exchange((up_weight, down_weight), "row", 1)
    up_full = jnp.concatenate([up_weight[0], partner_up[0]], axis=1)
    down_full = jnp.concatenate([down_weight[0], partner_down[0]], axis=0)
    outgoing = send_rows.reshape(experts * 2, capacity // 2, width)
    arrived = lax.all_to_all(outgoing, "row", split_axis=0, concat_axis=0, tiled=True)
    hidden = jax.nn.gelu(mxu(arrived.reshape(-1, width), up_full), approximate=True).astype(jnp.bfloat16)
    partial_out = mxu(hidden, down_full).reshape(arrived.shape).astype(jnp.bfloat16)
    returned = lax.all_to_all(partial_out, "row", split_axis=0, concat_axis=0, tiled=True)
    gathered = returned.reshape(-1, width)[slot_index].reshape(n_tokens, top_count, width)
    scaled = gathered.astype(jnp.float32) * combine.reshape(n_tokens, top_count, 1)
    return residual.astype(jnp.float32) + jnp.sum(scaled, axis=1)


def complex_weight(weight):
    real, imag = weight[0], weight[1]
    return jnp.concatenate(
        [jnp.concatenate([real, imag], axis=2), jnp.concatenate([-imag, real], axis=2)], axis=1
    )


def per_device(
    tokens,
    ln_first,
    spec_first,
    spec_second,
    spec_bias,
    ln_second,
    routing,
    combine,
    up_weight,
    down_weight,
):
    _, rows_local, grid_len, width = tokens.shape
    axes = ("row", "expert")
    n_dev = lax.axis_size(axes)
    n_blocks = spec_first.shape[1]
    forward_cols, inverse_cols = column_tables(grid_len, n_dev, rows_local)
    forward_rows, inverse_rows = row_tables(grid_len)
    first_device = lax.axis_index(axes) == 0
    pick = lambda table: jnp.stack([jnp.where(first_device, table[0], table[1]), table[1]])
    flat_tokens = tokens.reshape(-1, width)

    spectra = column_spectra(flat_tokens, ln_first.reshape(1, width), jnp.asarray(forward_cols))
    by_column = lax.all_to_all(
        spectra.reshape(n_dev, -1, spectra.shape[1]), axes, split_axis=0, concat_axis=0, tiled=True
    )
    bias = spec_bias.reshape(2, n_blocks, -1).transpose(1, 0, 2).reshape(n_blocks, -1)
    gain = ln_second.reshape(1, width)
    pairs = lax.axis_size("group") == 2 and lax.axis_size("expert") == 2
    every_expert = lax.axis_size("row") == 2 * routing.shape[-1] and routing.shape[-1] == 4
    dense = pairs and every_expert
    if dense:
        weights = Weights(up_weight[0], down_weight[0])
        table = expert_weights(routing, combine, routing.shape[-1])
        half_size = table.shape[1] // 2
        arriving = [exchange(table[:, :half_size], "row", 1), exchange(table[:, half_size:], "row", 2)]
        near = exchange(weights.part, "row", 3)
        far_up = exchange(weights.part[0], "row", 4)
        bias = gate(bias, far_up, *near)
    mixed = mix_modes(
        by_column.reshape(spectra.shape),
        pick(forward_rows),
        complex_weight(spec_first),
        complex_weight(spec_second),
        bias,
        pick(inverse_rows),
        width,
    )
    by_row = lax.all_to_all(
        mixed.reshape(n_dev, -1, mixed.shape[1]), axes, split_axis=0, concat_axis=0, tiled=True
    )
    if dense:
        near_all = Weights.spread(near)
        far_down = exchange(weights.part[1], "row", 4)
        far_near_up = exchange(far_up, "row", 3)
        gain = gate(gain, far_down, far_near_up, *near_all[0], *near_all[1], *arriving)
    residual, *norms = add_mixing(
        by_row.reshape(mixed.shape), jnp.asarray(inverse_cols), flat_tokens, gain
    )
    if not dense:
        normed = jnp.concatenate(norms)
        final = routed_experts(residual, normed, routing, combine, up_weight, down_weight)
        return final.astype(jnp.bfloat16).reshape(tokens.shape)

    per_row = len(norms) // 2
    rows_of = [1] * per_row + [2] * per_row
    others = [exchange(norm, "row", mask) for norm, mask in zip(norms, rows_of)]
    far_near_down = exchange(tie(far_down, mixed), "row", 3)
    far_all = Weights.spread((far_up, far_down))
    far_near_all = Weights.spread((far_near_up, far_near_down))
    expert = lax.axis_index("row") // 2
    pick_weights = lambda columns, numbers: jnp.stack(
        [lax.dynamic_index_in_dim(columns, expert ^ number, 0, keepdims=False) for number in numbers], axis=1
    )
    lower, upper = [weights.own, near_all], [far_all, far_near_all]
    (own,) = run_experts(norms, pick_weights(table, (0, 1)), lower)
    backs = [None] * len(norms)
    size = norms[0].shape[0]
    for index in range(per_row):
        sets = (index, index + per_row)
        table_in = jnp.concatenate([side[:, index * size : (index + 1) * size] for side in arriving], axis=1)
        results = run_experts([others[k] for k in sets], pick_weights(table_in, (0, 1, 2, 3)), lower + upper, split=True)
        for k, result in zip(sets, results):
            backs[k] = exchange(result, "row", rows_of[k])
    (own,) = run_experts(norms, pick_weights(table, (2, 3)), upper, [own])
    return add_outputs(residual, own, backs).reshape(tokens.shape)


def solution(mesh):
    placed = (
        P("group", ("row", "expert"), None, None),
        P(),
        P(),
        P(),
        P(),
        P(),
        P("group", ("row", "expert"), None, None),
        P("group", ("row", "expert"), None, None),
        P("row", None, None),
        P("row", None, None),
    )
    return jax.shard_map(
        per_device,
        mesh=mesh,
        in_specs=placed,
        out_specs=P("group", ("row", "expert"), None, None),
        check_vma=False,
    )
```

```python
import functools
import math

import jax
import jax.numpy as jnp
import ml_dtypes
import numpy as np
from jax import lax
from jax.experimental import pallas as pl
from jax.experimental.pallas import tpu as pltpu
from jax.sharding import PartitionSpec as P

MIB = 1 << 20


def exchange(value, axis, mask):
    pairs = [(source, source ^ mask) for source in range(lax.axis_size(axis))]
    return lax.ppermute(value, axis, pairs)


def mxu(left, right):
    return jnp.dot(left, right, preferred_element_type=jnp.float32)


def normalize(values, gain):
    center = values - jnp.mean(values, axis=-1, keepdims=True)
    spread = jnp.mean(center * center, axis=-1, keepdims=True)
    return center * lax.rsqrt(spread + 1e-05) * gain


def trig(grid_len):
    counter = np.arange(grid_len)
    angle = 2.0 * math.pi / grid_len * (np.outer(counter, counter) % grid_len)
    cosine = np.round(np.cos(angle), 12).astype(ml_dtypes.bfloat16).astype(np.float64)
    sine = np.round(np.sin(angle), 12).astype(ml_dtypes.bfloat16).astype(np.float64)
    return cosine, sine


def column_tables(grid_len, n_dev, rows_local):
    cosine, sine = trig(grid_len)
    packed = grid_len // 2
    per_dev = packed // n_dev
    part = np.stack([cosine[:packed], -sine[:packed]], axis=1)
    part[0, 1] = cosine[packed]
    part = part.reshape(n_dev, per_dev, 2, grid_len)
    forward = np.zeros((per_dev, n_dev, rows_local, 2, rows_local, grid_len))
    for row in range(rows_local):
        forward[:, :, row, :, row, :] = part.transpose(1, 0, 2, 3)
    forward = forward.reshape(per_dev, n_dev * rows_local * 2, rows_local * grid_len)
    inverse = forward.transpose(0, 2, 1) / grid_len
    return forward.astype(ml_dtypes.bfloat16), inverse.astype(ml_dtypes.bfloat16)


def row_tables(grid_len):
    c, s = trig(grid_len)
    z = np.zeros_like(c)

    def assemble(blocks):
        array = np.array(blocks)
        return array.transpose(0, 1, 3, 4, 2).reshape(4 * grid_len, 2 * grid_len)

    plain_fwd = assemble([[[c, s], [-s, c]], [[c, -s], [-s, -c]]]) / grid_len
    first_fwd = assemble([[[c, z], [-s, z]], [[z, c], [z, -s]]]) / grid_len
    plain_inv = assemble([[[c, s], [-s, c]], [[c, -s], [-s, -c]]]).T
    first_inv = assemble([[[c, z], [-s, z]], [[z, c], [z, -s]]]).T
    kinds = lambda first, plain: np.stack([first, plain]).astype(ml_dtypes.bfloat16)
    return kinds(first_fwd, plain_fwd), kinds(first_inv, plain_inv)


def spectra_kernel(tokens, gain, table, out, normed):
    tile = 128
    width = tokens.shape[1]

    def norm_tile(index, carry):
        rows = pl.ds(pl.multiple_of(index * tile, tile), tile)
        values = tokens[rows, :].astype(jnp.float32)
        normed[rows, :] = normalize(values, gain[...]).astype(normed.dtype)
        return carry

    lax.fori_loop(0, tokens.shape[0] // tile, norm_tile, 0)
    for column in range(table.shape[0]):
        out[:, column * width : (column + 1) * width] = mxu(table[column], normed[...]).astype(out.dtype)


def column_spectra(tokens, gain, table):
    per_dev, rows_out, rows_in = table.shape
    width = tokens.shape[1]
    return pl.pallas_call(
        spectra_kernel,
        out_shape=jax.ShapeDtypeStruct((rows_out, per_dev * width), jnp.bfloat16),
        in_specs=[pl.BlockSpec(memory_space=pltpu.VMEM)] * 3,
        out_specs=pl.BlockSpec(memory_space=pltpu.VMEM),
        scratch_shapes=[pltpu.VMEM((rows_in, width), jnp.bfloat16)],
        compiler_params=pltpu.CompilerParams(vmem_limit_bytes=20 * MIB),
        cost_estimate=pl.CostEstimate(
            flops=2 * per_dev * rows_out * rows_in * width,
            bytes_accessed=2 * (rows_in * width + rows_out * per_dev * width + table.size),
            transcendentals=0,
        ),
        name="column_spectra",
    )(tokens, gain, table)


def modes_kernel(spectra, forward, first, second, bias, inverse, out, mixed):
    n_blocks, pair, _ = first.shape
    block = pair // 2
    grid_len = spectra.shape[0] // 2
    modes = mxu(forward[0], spectra[...]).astype(jnp.bfloat16)
    for index in range(n_blocks):
        lanes = slice(index * block, (index + 1) * block)
        sides = [
            jnp.concatenate(
                [
                    modes[2 * sign * grid_len : (2 * sign + 1) * grid_len, lanes],
                    modes[(2 * sign + 1) * grid_len : (2 * sign + 2) * grid_len, lanes],
                ],
                axis=1,
            )
            for sign in range(2)
        ]
        hid = mxu(jnp.concatenate(sides, axis=0), first[index])
        hid = jnp.maximum(hid + bias[index : index + 1, :], 0.0).astype(jnp.bfloat16)
        result = mxu(hid, second[index]).astype(jnp.bfloat16)
        for sign in range(2):
            for part in range(2):
                base = (2 * sign + part) * grid_len
                mixed[base : base + grid_len, lanes] = result[
                    sign * grid_len : (sign + 1) * grid_len, part * block : (part + 1) * block
                ]
    out[...] = mxu(inverse[0], mixed[...]).astype(out.dtype)


def mix_modes(spectra, forward, first, second, bias, inverse, width):
    rows, lanes = spectra.shape
    per_dev = lanes // width
    modes_rows = forward.shape[1]
    kind = lambda k: (jnp.minimum(k, 1), 0, 0)
    whole3 = lambda k: (0, 0, 0)
    return pl.pallas_call(
        modes_kernel,
        grid=(per_dev,),
        out_shape=jax.ShapeDtypeStruct((rows, lanes), jnp.bfloat16),
        in_specs=[
            pl.BlockSpec((rows, width), lambda k: (0, k)),
            pl.BlockSpec((1,) + forward.shape[1:], kind),
            pl.BlockSpec(first.shape, whole3),
            pl.BlockSpec(second.shape, whole3),
            pl.BlockSpec(bias.shape, lambda k: (0, 0)),
            pl.BlockSpec((1,) + inverse.shape[1:], kind),
        ],
        out_specs=pl.BlockSpec((rows, width), lambda k: (0, k)),
        scratch_shapes=[pltpu.VMEM((modes_rows, width), jnp.bfloat16)],
        compiler_params=pltpu.CompilerParams(vmem_limit_bytes=20 * MIB),
        cost_estimate=pl.CostEstimate(
            flops=2 * lanes * (2 * rows * modes_rows + modes_rows * 512),
            bytes_accessed=4 * (rows * lanes + first.size),
            transcendentals=0,
        ),
        name="mix_modes",
    )(spectra, forward, first, second, bias, inverse)


def residual_kernel(spectra, table, tokens, gain, residual, *halves):
    width = tokens.shape[1]
    mixing = None
    for column in range(table.shape[0]):
        term = mxu(table[column], spectra[:, column * width : (column + 1) * width])
        mixing = term if mixing is None else mixing + term
    rounded = (tokens[...].astype(jnp.float32) + mixing).astype(jnp.bfloat16)
    residual[...] = rounded
    normed = normalize(rounded.astype(jnp.float32), gain[...]).astype(jnp.bfloat16)
    per_half = pl.num_programs(0) // len(halves)
    for index, half in enumerate(halves):

        @pl.when(pl.program_id(0) // per_half == index)
        def _(half=half):
            half[...] = normed


def part_tiles(tile, width, per_part, n_parts):
    return [
        pl.BlockSpec((tile, width), lambda i, first=index * per_part: (jnp.clip(i - first, 0, per_part - 1), 0))
        for index in range(n_parts)
    ]


def add_mixing(spectra, table, tokens, gain, n_parts=4):
    per_dev, rows_out, rows_in = table.shape
    width = tokens.shape[1]
    tile = math.gcd(rows_out // n_parts, 256)
    steps = rows_out // tile
    row_tile = pl.BlockSpec((tile, width), lambda i: (i, 0))
    return pl.pallas_call(
        residual_kernel,
        grid=(steps,),
        out_shape=[jax.ShapeDtypeStruct((rows, width), jnp.bfloat16) for rows in [rows_out] + n_parts * [rows_out // n_parts]],
        in_specs=[
            pl.BlockSpec(spectra.shape, lambda i: (0, 0)),
            pl.BlockSpec((per_dev, tile, rows_in), lambda i: (0, i, 0)),
            row_tile,
            pl.BlockSpec(gain.shape, lambda i: (0, 0)),
        ],
        out_specs=[row_tile] + part_tiles(tile, width, steps // n_parts, n_parts),
        compiler_params=pltpu.CompilerParams(vmem_limit_bytes=20 * MIB),
        cost_estimate=pl.CostEstimate(
            flops=2 * per_dev * rows_out * rows_in * width,
            bytes_accessed=2 * (3 * rows_out * width + spectra.size + table.size),
            transcendentals=0,
        ),
        name="add_mixing",
    )(spectra, table, tokens, gain)


def sum_kernel(residual, own, *refs):
    backs, out = refs[:-1], refs[-1]
    total = residual[...].astype(jnp.float32) + own[...]
    per_part = pl.num_programs(0) // len(backs)
    for index, back in enumerate(backs):

        @pl.when(pl.program_id(0) // per_part == index)
        def _(back=back):
            out[...] = (total + back[...].astype(jnp.float32)).astype(out.dtype)


def add_outputs(residual, own, backs):
    rows, width = residual.shape
    tile = math.gcd(rows // len(backs), 256)
    row_tile = pl.BlockSpec((tile, width), lambda i: (i, 0))
    return pl.pallas_call(
        sum_kernel,
        grid=(rows // tile,),
        out_shape=jax.ShapeDtypeStruct(residual.shape, jnp.bfloat16),
        in_specs=[row_tile, row_tile] + part_tiles(tile, width, rows // tile // len(backs), len(backs)),
        out_specs=row_tile,
        compiler_params=pltpu.CompilerParams(vmem_limit_bytes=16 * MIB),
        name="add_outputs",
    )(residual, own, *backs)


def gate(value, *others):
    anywhere = pl.BlockSpec(memory_space=pl.ANY)
    return pl.pallas_call(
        lambda *refs: None,
        out_shape=jax.ShapeDtypeStruct(value.shape, value.dtype),
        in_specs=[anywhere] * (1 + len(others)),
        out_specs=anywhere,
        input_output_aliases={0: 0},
        compiler_params=pltpu.CompilerParams(vmem_limit_bytes=MIB),
        cost_estimate=pl.CostEstimate(flops=10**11, bytes_accessed=10**8, transcendentals=0),
        name="gate",
    )(value, *others)


def gelu_twice(values):
    scale = math.sqrt(2.0 / math.pi)
    return values * jnp.tanh(values * (values * values * (0.044715 * scale) + scale)) + values


def experts_kernel(pieces, n_sets, n_outs, n_totals, chunk, weights, *refs):
    take = iter(refs)
    sets = [next(take) for _ in range(n_sets)]
    totals = [next(take) for _ in range(n_totals)]
    halves = [[next(take) for _ in range(count)] for count in pieces]
    outs = [next(take) for _ in range(n_outs)]
    values, up_all, down_all, set_sem, total_sem, piece_sem = (next(take) for _ in range(6))
    total = outs[0] if n_outs == 1 else next(take)
    n_blocks, _, hidden = up_all.shape
    tile = math.gcd(values.shape[0], 512)
    set_size = values.shape[0] // n_sets
    rows_of = lambda index: pl.ds(index * set_size, set_size)
    loads = [
        pltpu.make_async_copy(ref, values.at[rows_of(index)], set_sem.at[index]) for index, ref in enumerate(sets)
    ]
    total_loads = [
        pltpu.make_async_copy(ref, total.at[pl.ds(index * ref.shape[0], ref.shape[0])], total_sem.at[index])
        for index, ref in enumerate(totals)
    ]
    blocks = []
    piece = 0
    for block in range(n_blocks):
        copies = []
        for side in range(2):
            base = 0
            for ref in halves[2 * block + side]:
                size = ref.shape[1 - side]
                units = pl.ds(base, size)
                target = down_all.at[block, units, :] if side else up_all.at[block, :, units]
                copies.append(pltpu.make_async_copy(ref, target, piece_sem.at[piece]))
                base += size
                piece += 1
        blocks.append(copies)
    for copy in loads + blocks[0] + total_loads + blocks[1]:
        copy.start()
    for copy in loads:
        copy.wait()
    for block in range(n_blocks):
        for copy in blocks[block]:
            copy.wait()
        if 0 < block < n_blocks - 1:
            for copy in blocks[block + 1]:
                copy.start()
        if block == 0:
            for copy in total_loads:
                copy.wait()

        def token_tile(index, carry, block=block):
            rows = pl.ds(pl.multiple_of(index * tile, tile), tile)
            given = values[rows, :]
            acts = [
                gelu_twice(mxu(given, up_all[block, :, start : start + chunk])).astype(jnp.bfloat16)
                for start in range(0, hidden, chunk)
            ]
            term = mxu(jnp.concatenate(acts, axis=1), down_all[block]) * (0.5 * weights[rows, block : block + 1])
            if block > 0 or n_totals:
                term = total[rows, :] + term
            total[rows, :] = term
            return carry

        lax.fori_loop(0, values.shape[0] // tile, token_tile, 0)
    if n_outs > 1:
        for index, out in enumerate(outs):
            out[...] = total[index * set_size : (index + 1) * set_size, :].astype(out.dtype)


def run_experts(sets, weights, blocks, totals=(), split=False, chunk=256):
    rows, width = sets[0].shape
    halves = [half for block in blocks for half in block]
    weights_in = [piece for half in halves for piece in half]
    n_blocks = len(blocks)
    hidden = sum(piece.shape[1] for piece in blocks[0][0])
    chunk = math.gcd(chunk, hidden)
    n_rows = rows * len(sets)
    vmem = pl.BlockSpec(memory_space=pltpu.VMEM)
    anywhere = pl.BlockSpec(memory_space=pl.ANY)
    if split:
        out_shape = [jax.ShapeDtypeStruct((rows, width), jnp.bfloat16)] * len(sets)
    else:
        out_shape = [jax.ShapeDtypeStruct((n_rows, width), jnp.float32)]
    counts = tuple(len(half) for half in halves)
    used = n_blocks * 4 * width * hidden + 2 * n_rows * width + 4 * n_rows * width + (2 * n_rows * width if split else 0)
    return pl.pallas_call(
        functools.partial(experts_kernel, counts, len(sets), len(out_shape), len(totals), chunk),
        out_shape=out_shape,
        in_specs=[vmem] + [anywhere] * (len(sets) + len(totals) + len(weights_in)),
        out_specs=[vmem] * len(out_shape),
        scratch_shapes=[
            pltpu.VMEM((n_rows, width), jnp.bfloat16),
            pltpu.VMEM((n_blocks, width, hidden), jnp.bfloat16),
            pltpu.VMEM((n_blocks, hidden, width), jnp.bfloat16),
            pltpu.SemaphoreType.DMA((len(sets),)),
            pltpu.SemaphoreType.DMA((len(sets),)),
            pltpu.SemaphoreType.DMA((len(weights_in),)),
        ]
        + ([pltpu.VMEM((n_rows, width), jnp.float32)] if split else []),
        compiler_params=pltpu.CompilerParams(vmem_limit_bytes=used + 4 * MIB),
        cost_estimate=pl.CostEstimate(
            flops=4 * n_rows * width * hidden * n_blocks,
            bytes_accessed=4 * width * hidden * n_blocks + 8 * n_rows * width,
            transcendentals=n_rows * hidden * n_blocks,
        ),
        name="experts",
    )(weights, *sets, *totals, *weights_in)


def expert_weights(routing, combine, n_experts):
    route, weight = (value.reshape(-1, value.shape[-1]) for value in (routing, combine))
    return jnp.stack([jnp.sum(jnp.where(route == e, weight, 0.0), axis=-1) for e in range(n_experts)])


def tie(value, *others):
    return lax.optimization_barrier((value, others))[0]


class Weights:
    def __init__(self, up, down):
        n_parts = lax.axis_size("group") * lax.axis_size("expert")
        part = lax.axis_index("group") * lax.axis_size("expert") + lax.axis_index("expert")
        size = up.shape[1] // n_parts
        self.own = ([up], [down])
        self.part = (
            lax.dynamic_slice_in_dim(up, part * size, size, axis=1),
            lax.dynamic_slice_in_dim(down, part * size, size, axis=0),
        )

    @staticmethod
    def spread(piece):
        other = exchange(piece, "group", 1)
        pieces = [piece, other, exchange(piece, "expert", 1), exchange(other, "expert", 1)]
        return tuple(list(side) for side in zip(*pieces))


def routed_experts(residual, normed, routing, combine, up_weight, down_weight):
    n_tokens, width = normed.shape
    top_count = routing.shape[-1]
    experts = lax.axis_size("row") // 2
    capacity = n_tokens * top_count // experts
    flat_route = routing.reshape(-1)
    one_hot = (flat_route[:, None] == jnp.arange(experts, dtype=jnp.int32)[None, :]).astype(jnp.int32)
    earlier = jnp.cumsum(one_hot, axis=0) - one_hot
    slot_index = flat_route * capacity + jnp.sum(earlier * one_hot, axis=1)
    token_of = jnp.arange(n_tokens * top_count, dtype=jnp.int32) // top_count
    source_row = jnp.zeros((experts * capacity,), jnp.int32).at[slot_index].set(token_of)
    send_rows = normed[source_row].reshape(experts, capacity, width)
    partner_up, partner_down = exchange((up_weight, down_weight), "row", 1)
    up_full = jnp.concatenate([up_weight[0], partner_up[0]], axis=1)
    down_full = jnp.concatenate([down_weight[0], partner_down[0]], axis=0)
    outgoing = send_rows.reshape(experts * 2, capacity // 2, width)
    arrived = lax.all_to_all(outgoing, "row", split_axis=0, concat_axis=0, tiled=True)
    hidden = jax.nn.gelu(mxu(arrived.reshape(-1, width), up_full), approximate=True).astype(jnp.bfloat16)
    partial_out = mxu(hidden, down_full).reshape(arrived.shape).astype(jnp.bfloat16)
    returned = lax.all_to_all(partial_out, "row", split_axis=0, concat_axis=0, tiled=True)
    gathered = returned.reshape(-1, width)[slot_index].reshape(n_tokens, top_count, width)
    scaled = gathered.astype(jnp.float32) * combine.reshape(n_tokens, top_count, 1)
    return residual.astype(jnp.float32) + jnp.sum(scaled, axis=1)


def complex_weight(weight):
    real, imag = weight[0], weight[1]
    return jnp.concatenate(
        [jnp.concatenate([real, imag], axis=2), jnp.concatenate([-imag, real], axis=2)], axis=1
    )


def per_device(
    tokens,
    ln_first,
    spec_first,
    spec_second,
    spec_bias,
    ln_second,
    routing,
    combine,
    up_weight,
    down_weight,
):
    _, rows_local, grid_len, width = tokens.shape
    axes = ("row", "expert")
    n_dev = lax.axis_size(axes)
    n_blocks = spec_first.shape[1]
    forward_cols, inverse_cols = column_tables(grid_len, n_dev, rows_local)
    forward_rows, inverse_rows = row_tables(grid_len)
    first_device = lax.axis_index(axes) == 0
    pick = lambda table: jnp.stack([jnp.where(first_device, table[0], table[1]), table[1]])
    flat_tokens = tokens.reshape(-1, width)

    spectra = column_spectra(flat_tokens, ln_first.reshape(1, width), jnp.asarray(forward_cols))
    by_column = lax.all_to_all(
        spectra.reshape(n_dev, -1, spectra.shape[1]), axes, split_axis=0, concat_axis=0, tiled=True
    )
    bias = spec_bias.reshape(2, n_blocks, -1).transpose(1, 0, 2).reshape(n_blocks, -1)
    gain = ln_second.reshape(1, width)
    pairs = lax.axis_size("group") == 2 and lax.axis_size("expert") == 2
    every_expert = lax.axis_size("row") == 2 * routing.shape[-1] and routing.shape[-1] == 4
    dense = pairs and every_expert
    if dense:
        weights = Weights(up_weight[0], down_weight[0])
        table = expert_weights(routing, combine, routing.shape[-1])
        half_size = table.shape[1] // 2
        near = exchange(weights.part, "row", 3)
        far_up = exchange(weights.part[0], "row", 4)
        bias = gate(bias, far_up, *near)
    mixed = mix_modes(
        by_column.reshape(spectra.shape),
        pick(forward_rows),
        complex_weight(spec_first),
        complex_weight(spec_second),
        bias,
        pick(inverse_rows),
        width,
    )
    by_row = lax.all_to_all(
        mixed.reshape(n_dev, -1, mixed.shape[1]), axes, split_axis=0, concat_axis=0, tiled=True
    )
    if dense:
        near_all = Weights.spread(near)
        far_down = exchange(weights.part[1], "row", 4)
        far_near_up = exchange(far_up, "row", 3)
        late_table = tie(table, mixed)
        arriving = [exchange(late_table[:, :half_size], "row", 1), exchange(late_table[:, half_size:], "row", 2)]
        gain = gate(gain, far_down, far_near_up, *near_all[0], *near_all[1], *arriving)
    residual, *norms = add_mixing(
        by_row.reshape(mixed.shape), jnp.asarray(inverse_cols), flat_tokens, gain
    )
    if not dense:
        normed = jnp.concatenate(norms)
        final = routed_experts(residual, normed, routing, combine, up_weight, down_weight)
        return final.astype(jnp.bfloat16).reshape(tokens.shape)

    per_row = len(norms) // 2
    rows_of = [1] * per_row + [2] * per_row
    others = [exchange(norm, "row", mask) for norm, mask in zip(norms, rows_of)]
    far_near_down = exchange(tie(far_down, mixed), "row", 3)
    far_all = Weights.spread((far_up, far_down))
    far_near_all = Weights.spread((far_near_up, far_near_down))
    expert = lax.axis_index("row") // 2
    pick_weights = lambda columns, numbers: jnp.stack(
        [lax.dynamic_index_in_dim(columns, expert ^ number, 0, keepdims=False) for number in numbers], axis=1
    )
    lower, upper = [weights.own, near_all], [far_all, far_near_all]
    (own,) = run_experts(norms, pick_weights(table, (0, 1)), lower)
    backs = [None] * len(norms)
    size = norms[0].shape[0]
    for index in range(per_row):
        sets = (index, index + per_row)
        table_in = jnp.concatenate([side[:, index * size : (index + 1) * size] for side in arriving], axis=1)
        results = run_experts([others[k] for k in sets], pick_weights(table_in, (0, 1, 2, 3)), lower + upper, split=True)
        for k, result in zip(sets, results):
            backs[k] = exchange(result, "row", rows_of[k])
    (own,) = run_experts(norms, pick_weights(table, (2, 3)), upper, [own])
    return add_outputs(residual, own, backs).reshape(tokens.shape)


def solution(mesh):
    placed = (
        P("group", ("row", "expert"), None, None),
        P(),
        P(),
        P(),
        P(),
        P(),
        P("group", ("row", "expert"), None, None),
        P("group", ("row", "expert"), None, None),
        P("row", None, None),
        P("row", None, None),
    )
    return jax.shard_map(
        per_device,
        mesh=mesh,
        in_specs=placed,
        out_specs=P("group", ("row", "expert"), None, None),
        check_vma=False,
    )
```
